512 devices in a mesh: layer: 16 (over z), row: 8 (over x, core), col: 4 (over y).
Axes of the slice: x: 4, y: 4, z: 16, core: 2. Of those that a mesh axis runs over, the one named last changes fastest.
Arguments:
- graph: float32 [16384, 4096], P('layer', ('row', 'col')), as said below
- pattern: int32 [128, 32], P('layer', ('row', 'col')), may hold values 0 or 1
Outputs:
- expanded: float32 [4096, 4096], P(('row', 'layer'), 'col')
The draws below stay inside these ranges and needn't reach their ends.
Inputs may be any that keep to these rules, and one draw needn't show every extreme that they name: `graph`: every edge weight is nonnegative.
All inputs are finite; a program needn't handle non-finite values. No bound on the sum of `pattern` on one device may be relied on, other than what follows from the above.
Results may differ from the reference program's by a relative error of at most 0.00005.
Values sent between devices are 32-bit elements; how exact they have to be, the bound alone decides.
No kernel may reach another device: no remote copies, remote signals or barrier semaphores. Data moves between devices by JAX's collectives and lax.ppermute only.
A program may use at most 64 MiB of HBM per device.

```python
import jax
import jax.numpy as jnp
from jax import lax

TILE = 128
K_ALL = 16384
N = 4096
N_ROW = 8
N_COL = 4


def draw_graph(key, part):
    key = jax.random.fold_in(key, 11)
    unit = jax.random.uniform(key, (K_ALL, N), jnp.float32)
    return unit * jnp.sqrt(6.0 / K_ALL)


def plant(array, rng, low, top_value):
    longest = array.shape.index(max(array.shape))
    spots = []
    for shift in (0, 1):
        where = [jax.random.randint(jax.random.fold_in(rng, axis), (), 0, length) for axis, length in enumerate(array.shape)]
        where[longest] = (where[longest] + shift) % array.shape[longest]
        spots.append(tuple(where))
    return array.at[spots[0]].set(low).at[spots[1]].set(top_value)


def setup_inputs(seed: int = 0) -> dict:
    key_list = jax.random.split(jax.random.key(seed), 3)
    return {
        "graph": draw_graph(jax.random.fold_in(key_list[2], 71), 0),
        "pattern": plant((jax.random.randint(key_list[1], (K_ALL // TILE, N // TILE), 0, 2) < 1).astype(jnp.int32), jax.random.fold_in(key_list[1], 1), 0, 1),
    }


def reference(graph, pattern):
    occupied = jnp.repeat(jnp.repeat(pattern.astype(jnp.float32), TILE, 0), TILE, 1)
    masked = graph * occupied
    flow = jnp.dot(masked.T, masked, precision=lax.Precision.HIGHEST, preferred_element_type=jnp.float32)
    reordered = flow.reshape(N, N_ROW, N_COL, TILE).transpose(0, 2, 1, 3).reshape(N, N)
    return reordered
```

```python
import functools

import jax
import jax.numpy as jnp
from jax import lax
from jax.experimental import pallas as pl
from jax.experimental.pallas import tpu as pltpu
from jax.sharding import PartitionSpec as P

TILE = 128
N_LAYER = 16
N_X = 4
N_COL = 4
SUB = 32
VMEM = pl.BlockSpec(memory_space=pltpu.VMEM)
SMEM = pl.BlockSpec(memory_space=pltpu.SMEM)
LIMIT = 40 * 1024 * 1024


def call(kernel, outs, operands, specs=None, scratch=(), flops=0, nbytes=1 << 20):
    return pl.pallas_call(
        kernel,
        out_shape=tuple(jax.ShapeDtypeStruct(s, jnp.float32) for s in outs),
        in_specs=specs or [VMEM] * len(operands),
        out_specs=tuple(VMEM for _ in outs),
        scratch_shapes=list(scratch),
        compiler_params=pltpu.CompilerParams(vmem_limit_bytes=LIMIT),
        cost_estimate=pl.CostEstimate(flops=flops, bytes_accessed=nbytes, transcendentals=0),
    )(*operands)


def mask_kernel(graph, pattern, masked, turned):
    for k in range(graph.shape[0] // TILE):
        rows = pl.ds(k * TILE, TILE)
        block = graph[rows, :] * pattern[k].astype(jnp.float32)
        masked[rows, :] = block
        turned[:, rows] = block.T


def split(value):
    high = value.astype(jnp.bfloat16)
    low = (value - high.astype(jnp.float32)).astype(jnp.bfloat16)
    return high, low


def product_kernel(*refs):
    lefts, rights, others = refs[:4], refs[4:8], refs[8:12]
    own, up, down, far_a, far_b = refs[12:17]
    left_high, left_low, total = refs[17:]
    z, row, y = lax.axis_index("layer"), lax.axis_index("row"), lax.axis_index("col")
    for t in range(4):
        rows = pl.ds(t * TILE, TILE)
        left_high[rows, :], left_low[rows, :] = split(lefts[t][...])

    for t in range(4):
        right = jnp.concatenate([rights[t][...], others[t][...]], axis=1)
        high, low = split(right)
        dot = functools.partial(jnp.dot, preferred_element_type=jnp.float32)
        block = dot(left_high[...], high) + (dot(left_high[...], low) + dot(left_low[...], high))
        q = lax.rem(row + 2 * t, 2 * N_X)
        partner = q + 1 - 2 * lax.rem(q, 2)
        total[:, pl.ds(pl.multiple_of(q * TILE, TILE), TILE)] = block[:, :TILE]
        total[:, pl.ds(pl.multiple_of(partner * TILE, TILE), TILE)] = block[:, TILE:]

    for c in range(N_COL):
        t = lax.rem(c - y + N_COL, N_COL)

        def strip(shift):
            return pl.ds(pl.multiple_of(t * TILE + lax.rem(z + shift, 4) * SUB, SUB), SUB)

        rows = pl.ds(c * SUB, SUB)
        half = total.shape[1] // 2
        own[rows, :] = total[strip(0), :]
        up[rows, :] = total[strip(1), :]
        down[rows, :] = total[strip(3), :]
        far_a[rows, :] = total[strip(2), :half]
        far_b[rows, :] = total[strip(2), half:]


def near_sum_kernel(own, up, down, far_a, far_b, *outs):
    home = lax.axis_index("layer") // 4
    half = own.shape[1] // 2
    for shift in range(4):
        c = lax.rem(home + shift, 4)
        rows = pl.ds(pl.multiple_of(c * SUB, SUB), SUB)
        near = own[rows, :] + (up[rows, :] + down[rows, :])
        outs[shift][:, :half] = near[:, :half] + far_a[rows, :]
        outs[shift][:, half:] = near[:, half:] + far_b[rows, :]


def last_sum_kernel(a, b, c, d, out):
    out[...] = (a[...] + b[...]) + (c[...] + d[...])


def layers_up(value, shift):
    return lax.ppermute(value, "layer", [(i, (i + shift) % N_LAYER) for i in range(N_LAYER)])


def from_col(value, t):
    return lax.ppermute(value, "col", [((i + t) % N_COL, i) for i in range(N_COL)])


def from_chip(value, t):
    return lax.ppermute(
        value, "row", [(2 * ((x + t) % N_X) + k, 2 * x + k) for x in range(N_X) for k in range(2)]
    )


def swap(value):
    return lax.ppermute(value, "row", [(i, i ^ 1) for i in range(2 * N_X)])


def on_device(graph, pattern):
    inner = graph.shape[0]
    masked, turned = call(
        mask_kernel, [(inner, TILE), (TILE, inner)], (graph, pattern.reshape(-1)), [VMEM, SMEM]
    )
    lefts, rights, others = {0: turned}, {0: masked}, {}
    for t in (1, 3, 2):
        lefts[t] = from_col(turned, t)
        rights[t] = from_chip(masked, t)
    for t in (0, 1, 3, 2):
        others[t] = swap(rights[t])
    operands = [d[t] for d in (lefts, rights, others) for t in range(4)]
    rows, width = 4 * SUB, 8 * TILE
    sends = call(
        product_kernel,
        [(rows, width)] * 3 + [(rows, width // 2)] * 2,
        operands,
        scratch=[
            pltpu.VMEM((4 * TILE, inner), jnp.bfloat16),
            pltpu.VMEM((4 * TILE, inner), jnp.bfloat16),
            pltpu.VMEM((4 * TILE, width), jnp.float32),
        ],
        flops=6 * 512 * 1024 * 1024,
        nbytes=8 << 20,
    )
    own, up, down, far_a, far_b = sends
    chunks = call(
        near_sum_kernel,
        [(SUB, width)] * 4,
        (own, layers_up(up, 1), layers_up(down, -1), layers_up(far_a, -2), layers_up(far_b, 2)),
    )
    return call(
        last_sum_kernel,
        [(SUB, width)],
        (chunks[0], layers_up(chunks[1], 4), layers_up(chunks[3], -4), layers_up(chunks[2], 8)),
    )[0]


def solution(mesh):
    placed = (P("layer", ("row", "col")), P("layer", ("row", "col")))
    return jax.shard_map(
        on_device, mesh=mesh, in_specs=placed, out_specs=P(("row", "layer"), "col"), check_vma=False
    )
```

```python
import functools

import jax
import jax.numpy as jnp
from jax import lax
from jax.experimental import pallas as pl
from jax.experimental.pallas import tpu as pltpu
from jax.sharding import PartitionSpec as P

TILE = 128
N_LAYER = 16
N_X = 4
N_ROW = 8
N_COL = 4
SUB = 32
ORDER = (0, 1, 3, 2)
VMEM = pl.BlockSpec(memory_space=pltpu.VMEM)
SMEM = pl.BlockSpec(memory_space=pltpu.SMEM)
LIMIT = 40 * 1024 * 1024
F32, BF16 = jnp.float32, jnp.bfloat16


def call(kernel, outs, operands, specs=None, scratch=(), flops=0, nbytes=1 << 20):
    outs = [o if isinstance(o[0], tuple) else (o, F32) for o in outs]
    return pl.pallas_call(
        kernel,
        out_shape=tuple(jax.ShapeDtypeStruct(s, d) for s, d in outs),
        in_specs=specs or [VMEM] * len(operands),
        out_specs=tuple(VMEM for _ in outs),
        scratch_shapes=list(scratch),
        compiler_params=pltpu.CompilerParams(vmem_limit_bytes=LIMIT),
        cost_estimate=pl.CostEstimate(flops=flops, bytes_accessed=nbytes, transcendentals=0),
    )(*operands)


def mask_kernel(graph, pattern, masked):
    for k in range(graph.shape[0] // TILE):
        rows = pl.ds(k * TILE, TILE)
        masked[rows, :] = graph[rows, :] * pattern[k].astype(F32)


def core():
    return lax.rem(lax.axis_index("row"), 2)


def pair_kernel(own, other, pair):
    inner = own.shape[0]
    k = core()
    pair[pl.ds(pl.multiple_of(k * inner, inner), inner), :] = own[...]
    pair[pl.ds(pl.multiple_of((1 - k) * inner, inner), inner), :] = other[...]


def split(value):
    high = value.astype(BF16)
    low = (value - high.astype(F32)).astype(BF16)
    return high, low


dot = functools.partial(jnp.dot, preferred_element_type=F32)


def product(left_high, left_low, right_high, right_low):
    return dot(left_high, right_high) + (dot(left_high, right_low) + dot(left_low, right_high))


def place(pair, swapped, along_y, along_x):
    k = core()

    @pl.when(k == 0)
    def _():
        along_y(pair)
        along_x(swapped)

    @pl.when(k == 1)
    def _():
        along_y(swapped)
        along_x(pair)


def take_left(index, left_high, left_low):
    def write(pair):
        inner = pair.shape[0] // 2
        block = pair[pl.ds(pl.multiple_of(core() * inner, inner), inner), :]
        rows = pl.ds(index * TILE, TILE)
        high, low = split(block.T)
        left_high[rows, :] = high
        left_low[rows, :] = low

    return write


def take_right(index, right_high, right_low):
    def write(pair):
        inner = pair.shape[0] // 2
        for k in range(2):
            columns = pl.ds((2 * index + k) * TILE, TILE)
            high, low = split(pair[pl.ds(k * inner, inner), :])
            right_high[:, columns] = high
            right_low[:, columns] = low

    return write


def first_product_kernel(p0, p1, s1, p3, s3, left_high, left_low, right_high, right_low, total):
    take_left(0, left_high, left_low)(p0)
    take_right(0, right_high, right_low)(p0)
    for index, pair, swapped in ((1, p1, s1), (2, p3, s3)):
        place(pair, swapped, take_left(index, left_high, left_low), take_right(index, right_high, right_low))
    for index in range(3):
        columns = pl.ds(index * 2 * TILE, 2 * TILE)
        total[:, columns] = product(left_high[...], left_low[...], right_high[:, columns], right_low[:, columns])


def turn():
    return 1 - 2 * core()


def strip(index):
    return pl.ds(pl.multiple_of(index * SUB, SUB), SUB)


def second_product_kernel(p2, s2, left_high, left_low, right_high, right_low, part, *refs):
    sends, keeps = refs[0:2], refs[2:4]
    last_high, last_low, far_high, far_low, total = refs[4:]
    z, y = lax.axis_index("layer"), lax.axis_index("col")
    place(p2, s2, take_left(0, last_high, last_low), take_right(0, far_high, far_low))
    known = part.shape[0]
    total[:known, : part.shape[1]] = part[...]
    total[known:, : part.shape[1]] = product(last_high[...], last_low[...], right_high[...], right_low[...])
    columns = pl.ds(part.shape[1], 2 * TILE)
    total[:known, columns] = product(left_high[...], left_low[...], far_high[...], far_low[...])
    total[known:, columns] = product(last_high[...], last_low[...], far_high[...], far_low[...])

    def rows_of(layer):
        t = lax.rem(layer // 4 - y + N_COL, N_COL)
        index = jnp.where(t < 2, t, 5 - t)
        return strip(index * 4 + lax.rem(layer, 4))

    for j in range(N_LAYER // 2):
        keep = rows_of(lax.rem(z + 2 * j, N_LAYER))
        send = rows_of(lax.rem(z + turn() + 2 * j + N_LAYER, N_LAYER))
        rows = pl.ds(j * SUB, SUB)
        for half in range(2):
            columns = pl.ds(half * 4 * TILE, 4 * TILE)
            keeps[half][rows, :] = total[keep, columns]
            sends[half][rows, :] = total[send, columns]


def stage_kernel(held, came, send, keep):
    count = held.shape[0] // SUB
    for i in range(count // 2):
        rows = pl.ds(i * SUB, SUB)
        near = pl.ds(2 * i * SUB, SUB)
        far = strip(lax.rem(turn() + 2 * i + count, count))
        keep[rows, :] = held[near, :] + came[near, :]
        send[rows, :] = held[far, :] + came[far, :]


def last_kernel(held_a, came_a, held_b, came_b, out):
    x = lax.axis_index("row") // 2
    for index, t in enumerate(ORDER):
        held, came = ((held_a, came_a), (held_b, came_b))[index // 2]
        source = pl.ds((index % 2) * 2 * TILE, 2 * TILE)
        target = pl.ds(pl.multiple_of(lax.rem(x + t, N_X) * 2 * TILE, 2 * TILE), 2 * TILE)
        out[:, target] = held[:, source] + came[:, source]


def swap(value):
    return lax.ppermute(value, "row", [(i, i ^ 1) for i in range(N_ROW)])


def fetch(value, t):
    pairs = []
    for x in range(N_X):
        for y in range(N_COL):
            pairs.append(((2 * x) * N_COL + (y + t) % N_COL, (2 * x) * N_COL + y))
            pairs.append(((2 * ((x + t) % N_X) + 1) * N_COL + y, (2 * x + 1) * N_COL + y))
    return lax.ppermute(value, ("row", "col"), pairs)


def pass_on(value, distance):
    pairs = []
    for z in range(N_LAYER):
        for row in range(N_ROW):
            to = (z + (distance if row % 2 == 0 else -distance)) % N_LAYER
            pairs.append((z * N_ROW + row, to * N_ROW + row))
    return lax.ppermute(value, ("layer", "row"), pairs)


def on_device(graph, pattern):
    inner = graph.shape[0]
    (masked,) = call(mask_kernel, [(inner, TILE)], (graph, pattern.reshape(-1)), [VMEM, SMEM])
    (pair,) = call(pair_kernel, [(2 * inner, TILE)], (masked, swap(masked)))
    came = {t: fetch(pair, t) for t in (1, 3, 2)}
    swapped = {t: swap(came[t]) for t in (1, 3, 2)}
    known, wide = 3 * TILE, 6 * TILE
    parts = call(
        first_product_kernel,
        [((known, inner), BF16)] * 2 + [((inner, wide), BF16)] * 2 + [(known, wide)],
        (pair, came[1], swapped[1], came[3], swapped[3]),
        flops=6 * known * wide * inner,
        nbytes=8 << 20,
    )
    split_scratch = [pltpu.VMEM((TILE, inner), BF16)] * 2 + [pltpu.VMEM((inner, 2 * TILE), BF16)] * 2
    made = call(
        second_product_kernel,
        [(8 * SUB, 4 * TILE)] * 4,
        (came[2], swapped[2], *parts),
        scratch=split_scratch + [pltpu.VMEM((4 * TILE, 8 * TILE), F32)],
        flops=6 * 7 * TILE * 2 * TILE * inner,
        nbytes=8 << 20,
    )
    sends, keeps = list(made[:2]), list(made[2:])
    arrived = [pass_on(sends[half], 1) for half in range(2)]
    for stage in (1, 2, 3):
        count = 8 >> stage
        for half in range(2):
            sends[half], keeps[half] = call(
                stage_kernel, [(count * SUB, 4 * TILE)] * 2, (keeps[half], arrived[half])
            )
            arrived[half] = pass_on(sends[half], 1 << stage)
    return call(last_kernel, [(SUB, 8 * TILE)], (keeps[0], arrived[0], keeps[1], arrived[1]))[0]


def solution(mesh):
    placed = (P("layer", ("row", "col")), P("layer", ("row", "col")))
    return jax.shard_map(
        on_device, mesh=mesh, in_specs=placed, out_specs=P(("row", "layer"), "col"), check_vma=False
    )
```

```python
import functools

import jax
import jax.numpy as jnp
from jax import lax
from jax.experimental import pallas as pl
from jax.experimental.pallas import tpu as pltpu
from jax.sharding import PartitionSpec as P

TILE = 128
N_LAYER = 16
N_X = 4
N_ROW = 8
N_COL = 4
SUB = 32
ORDER = (0, 1, 3, 2)
VMEM = pl.BlockSpec(memory_space=pltpu.VMEM)
SMEM = pl.BlockSpec(memory_space=pltpu.SMEM)
LIMIT = 40 * 1024 * 1024
F32, BF16 = jnp.float32, jnp.bfloat16


def call(kernel, outs, operands, specs=None, scratch=(), flops=0, nbytes=1 << 20):
    outs = [o if isinstance(o[0], tuple) else (o, F32) for o in outs]
    return pl.pallas_call(
        kernel,
        out_shape=tuple(jax.ShapeDtypeStruct(s, d) for s, d in outs),
        in_specs=specs or [VMEM] * len(operands),
        out_specs=tuple(VMEM for _ in outs),
        scratch_shapes=list(scratch),
        compiler_params=pltpu.CompilerParams(vmem_limit_bytes=LIMIT),
        cost_estimate=pl.CostEstimate(flops=flops, bytes_accessed=nbytes, transcendentals=0),
    )(*operands)


def mask_kernel(graph, pattern, masked):
    for k in range(graph.shape[0] // TILE):
        rows = pl.ds(k * TILE, TILE)
        masked[rows, :] = graph[rows, :] * pattern[k].astype(F32)


def core():
    return lax.rem(lax.axis_index("row"), 2)


def pair_kernel(own, other, pair):
    inner = own.shape[0]
    k = core()
    pair[pl.ds(pl.multiple_of(k * inner, inner), inner), :] = own[...]
    pair[pl.ds(pl.multiple_of((1 - k) * inner, inner), inner), :] = other[...]


def join_kernel(first, second, pair):
    inner = first.shape[0]
    pair[:inner, :] = first[...]
    pair[inner:, :] = second[...]


def split(value):
    high = value.astype(BF16)
    low = (value - high.astype(F32)).astype(BF16)
    return high, low


dot = functools.partial(jnp.dot, preferred_element_type=F32)


def product(left_high, left_low, right_high, right_low):
    return dot(left_high, right_high) + (dot(left_high, right_low) + dot(left_low, right_high))


def place(pair, swapped, along_y, along_x):
    k = core()

    @pl.when(k == 0)
    def _():
        along_y(pair)
        along_x(swapped)

    @pl.when(k == 1)
    def _():
        along_y(swapped)
        along_x(pair)


def take_left(index, left_high, left_low):
    def write(pair):
        inner = pair.shape[0] // 2
        block = pair[pl.ds(pl.multiple_of(core() * inner, inner), inner), :]
        rows = pl.ds(index * TILE, TILE)
        high, low = split(block.T)
        left_high[rows, :] = high
        left_low[rows, :] = low

    return write


def take_right(index, right_high, right_low):
    def write(pair):
        inner = pair.shape[0] // 2
        for k in range(2):
            columns = pl.ds((2 * index + k) * TILE, TILE)
            high, low = split(pair[pl.ds(k * inner, inner), :])
            right_high[:, columns] = high
            right_low[:, columns] = low

    return write


def first_product_kernel(p0, p1, s1, p3, s3, left_high, left_low, right_high, right_low, total):
    take_left(0, left_high, left_low)(p0)
    take_right(0, right_high, right_low)(p0)
    for index, pair, swapped in ((1, p1, s1), (2, p3, s3)):
        place(pair, swapped, take_left(index, left_high, left_low), take_right(index, right_high, right_low))
    for index in range(3):
        columns = pl.ds(index * 2 * TILE, 2 * TILE)
        total[:, columns] = product(left_high[...], left_low[...], right_high[:, columns], right_low[:, columns])


def turn():
    return 1 - 2 * core()


def strip(index):
    return pl.ds(pl.multiple_of(index * SUB, SUB), SUB)


def second_product_kernel(p2, s2, left_high, left_low, right_high, right_low, part, *refs):
    outs = refs[:8]
    last_high, last_low, far_high, far_low, total = refs[8:]
    z = lax.axis_index("layer")
    place(p2, s2, take_left(0, last_high, last_low), take_right(0, far_high, far_low))
    known = part.shape[0]
    total[:known, : part.shape[1]] = part[...]
    total[known:, : part.shape[1]] = product(last_high[...], last_low[...], right_high[...], right_low[...])
    columns = pl.ds(part.shape[1], 2 * TILE)
    total[:known, columns] = product(left_high[...], left_low[...], far_high[...], far_low[...])
    total[known:, columns] = product(last_high[...], last_low[...], far_high[...], far_low[...])
    for steps in range(4):
        s = lax.rem(z + turn() * steps + 4, 4)
        for half in range(2):
            for t in range(4):
                columns = pl.ds(half * 4 * TILE, 4 * TILE)
                outs[4 * half + steps][pl.ds(t * SUB, SUB), :] = total[strip(t * 4 + s), columns]


def add_kernel(held, came, out):
    out[...] = held[...] + came[...]


def near_end_kernel(held, came, *outs):
    group, y = lax.axis_index("layer") // 4, lax.axis_index("col")
    for steps in range(4):
        t = lax.rem(group + turn() * steps - y + 8, 4)
        rows = strip(jnp.where(t < 2, t, 5 - t))
        outs[steps][...] = held[rows, :] + came[rows, :]


def last_kernel(held_a, came_a, held_b, came_b, out):
    x = lax.axis_index("row") // 2
    for index, t in enumerate(ORDER):
        held, came = ((held_a, came_a), (held_b, came_b))[index // 2]
        source = pl.ds((index % 2) * 2 * TILE, 2 * TILE)
        target = pl.ds(pl.multiple_of(lax.rem(x + t, N_X) * 2 * TILE, 2 * TILE), 2 * TILE)
        out[:, target] = held[:, source] + came[:, source]


def swap(value):
    return lax.ppermute(value, "row", [(i, i ^ 1) for i in range(N_ROW)])


def fetch(value, t):
    pairs = []
    for x in range(N_X):
        for y in range(N_COL):
            pairs.append(((2 * x) * N_COL + (y + t) % N_COL, (2 * x) * N_COL + y))
            pairs.append(((2 * ((x + t) % N_X) + 1) * N_COL + y, (2 * x + 1) * N_COL + y))
    return lax.ppermute(value, ("row", "col"), pairs)


def pass_on(value, distance):
    pairs = []
    for z in range(N_LAYER):
        for row in range(N_ROW):
            to = (z + (distance if row % 2 == 0 else -distance)) % N_LAYER
            pairs.append((z * N_ROW + row, to * N_ROW + row))
    return lax.ppermute(value, ("layer", "row"), pairs)


def on_device(graph, pattern):
    inner = graph.shape[0]
    (masked,) = call(mask_kernel, [(inner, TILE)], (graph, pattern.reshape(-1)), [VMEM, SMEM])
    (pair,) = call(pair_kernel, [(2 * inner, TILE)], (masked, swap(masked)))
    came = {t: fetch(pair, t) for t in (1, 3)}
    far = (fetch(came[1][:inner], 1), fetch(came[3][inner:], 3))
    swapped = {t: swap(came[t]) for t in (1, 3)}
    known, wide = 3 * TILE, 6 * TILE
    parts = call(
        first_product_kernel,
        [((known, inner), BF16)] * 2 + [((inner, wide), BF16)] * 2 + [(known, wide)],
        (pair, came[1], swapped[1], came[3], swapped[3]),
        flops=6 * known * wide * inner,
        nbytes=8 << 20,
    )
    far, parts = lax.optimization_barrier((far, parts))
    (last,) = call(join_kernel, [(2 * inner, TILE)], far)
    split_scratch = [pltpu.VMEM((TILE, inner), BF16)] * 2 + [pltpu.VMEM((inner, 2 * TILE), BF16)] * 2
    made = call(
        second_product_kernel,
        [(4 * SUB, 4 * TILE)] * 8,
        (last, swap(last), *parts),
        scratch=split_scratch + [pltpu.VMEM((4 * TILE, 8 * TILE), F32)],
        flops=6 * 7 * TILE * 2 * TILE * inner,
        nbytes=8 << 20,
    )
    held = [made[:4], made[4:]]
    moving = [held[half][3] for half in range(2)]
    for steps in (2, 1):
        for half in range(2):
            operands = (held[half][steps], pass_on(moving[half], 1))
            (moving[half],) = call(add_kernel, [(4 * SUB, 4 * TILE)], operands)
    for half in range(2):
        operands = (held[half][0], pass_on(moving[half], 1))
        held[half] = call(near_end_kernel, [(SUB, 4 * TILE)] * 4, operands)
        moving[half] = held[half][3]
    for steps in (2, 1):
        for half in range(2):
            operands = (held[half][steps], pass_on(moving[half], 4))
            (moving[half],) = call(add_kernel, [(SUB, 4 * TILE)], operands)
    ends = [operand for half in range(2) for operand in (held[half][0], pass_on(moving[half], 4))]
    return call(last_kernel, [(SUB, 8 * TILE)], ends)[0]


def solution(mesh):
    placed = (P("layer", ("row", "col")), P("layer", ("row", "col")))
    return jax.shard_map(
        on_device, mesh=mesh, in_specs=placed, out_specs=P(("row", "layer"), "col"), check_vma=False
    )
```

```python
import functools

import jax
import jax.numpy as jnp
from jax import lax
from jax.experimental import pallas as pl
from jax.experimental.pallas import tpu as pltpu
from jax.sharding import PartitionSpec as P

TILE = 128
N_LAYER = 16
N_X = 4
N_ROW = 8
N_COL = 4
SUB = 32
ORDER = (0, 1, 3, 2)
VMEM = pl.BlockSpec(memory_space=pltpu.VMEM)
SMEM = pl.BlockSpec(memory_space=pltpu.SMEM)
LIMIT = 40 * 1024 * 1024
F32, BF16 = jnp.float32, jnp.bfloat16


def call(kernel, outs, operands, specs=None, scratch=(), flops=0, nbytes=1 << 20):
    outs = [o if isinstance(o[0], tuple) else (o, F32) for o in outs]
    return pl.pallas_call(
        kernel,
        out_shape=tuple(jax.ShapeDtypeStruct(s, d) for s, d in outs),
        in_specs=specs or [VMEM] * len(operands),
        out_specs=tuple(VMEM for _ in outs),
        scratch_shapes=list(scratch),
        compiler_params=pltpu.CompilerParams(vmem_limit_bytes=LIMIT),
        cost_estimate=pl.CostEstimate(flops=flops, bytes_accessed=nbytes, transcendentals=0),
    )(*operands)


def mask_kernel(graph, pattern, masked):
    for k in range(graph.shape[0] // TILE):
        rows = pl.ds(k * TILE, TILE)
        masked[rows, :] = graph[rows, :] * pattern[k].astype(F32)


def core():
    return lax.rem(lax.axis_index("row"), 2)


def pair_kernel(own, other, pair):
    inner = own.shape[0]
    k = core()
    pair[pl.ds(pl.multiple_of(k * inner, inner), inner), :] = own[...]
    pair[pl.ds(pl.multiple_of((1 - k) * inner, inner), inner), :] = other[...]


def join_kernel(first, second, pair):
    inner = first.shape[0]
    pair[:inner, :] = first[...]
    pair[inner:, :] = second[...]


def split(value):
    high = value.astype(BF16)
    low = (value - high.astype(F32)).astype(BF16)
    return high, low


dot = functools.partial(jnp.dot, preferred_element_type=F32)


def product(left_high, left_low, right_high, right_low):
    return dot(left_high, right_high) + (dot(left_high, right_low) + dot(left_low, right_high))


def place(pair, swapped, along_y, along_x):
    k = core()

    @pl.when(k == 0)
    def _():
        along_y(pair)
        along_x(swapped)

    @pl.when(k == 1)
    def _():
        along_y(swapped)
        along_x(pair)


def take_left(index, left_high, left_low):
    def write(pair):
        inner = pair.shape[0] // 2
        block = pair[pl.ds(pl.multiple_of(core() * inner, inner), inner), :]
        rows = pl.ds(index * TILE, TILE)
        high, low = split(block.T)
        left_high[rows, :] = high
        left_low[rows, :] = low

    return write


def take_right(index, right_high, right_low):
    def write(pair):
        inner = pair.shape[0] // 2
        for k in range(2):
            columns = pl.ds((2 * index + k) * TILE, TILE)
            high, low = split(pair[pl.ds(k * inner, inner), :])
            right_high[:, columns] = high
            right_low[:, columns] = low

    return write


def first_product_kernel(p0, p1, s1, p3, s3, left_high, left_low, right_high, right_low, total):
    take_left(0, left_high, left_low)(p0)
    take_right(0, right_high, right_low)(p0)
    for index, pair, swapped in ((1, p1, s1), (2, p3, s3)):
        place(pair, swapped, take_left(index, left_high, left_low), take_right(index, right_high, right_low))
    for index in range(3):
        columns = pl.ds(index * 2 * TILE, 2 * TILE)
        total[:, columns] = product(left_high[...], left_low[...], right_high[:, columns], right_low[:, columns])


def turn():
    return 1 - 2 * core()


def strip(index):
    return pl.ds(pl.multiple_of(index * SUB, SUB), SUB)


def second_product_kernel(p2, s2, left_high, left_low, right_high, right_low, part, *refs):
    sends, keeps = refs[0:2], refs[2:4]
    last_high, last_low, far_high, far_low, total = refs[4:]
    z, y = lax.axis_index("layer"), lax.axis_index("col")
    place(p2, s2, take_left(0, last_high, last_low), take_right(0, far_high, far_low))
    known = part.shape[0]
    total[:known, : part.shape[1]] = part[...]
    total[known:, : part.shape[1]] = product(last_high[...], last_low[...], right_high[...], right_low[...])
    columns = pl.ds(part.shape[1], 2 * TILE)
    total[:known, columns] = product(left_high[...], left_low[...], far_high[...], far_low[...])
    total[known:, columns] = product(last_high[...], last_low[...], far_high[...], far_low[...])

    def rows_of(layer):
        t = lax.rem(layer // 4 - y + N_COL, N_COL)
        index = jnp.where(t < 2, t, 5 - t)
        return strip(index * 4 + lax.rem(layer, 4))

    for j in range(N_LAYER // 2):
        keep = rows_of(lax.rem(z + 2 * j, N_LAYER))
        send = rows_of(lax.rem(z + turn() + 2 * j + N_LAYER, N_LAYER))
        rows = pl.ds(j * SUB, SUB)
        for half in range(2):
            columns = pl.ds(half * 4 * TILE, 4 * TILE)
            keeps[half][rows, :] = total[keep, columns]
            sends[half][rows, :] = total[send, columns]


def stage_kernel(held, came, send, keep):
    count = held.shape[0] // SUB
    for i in range(count // 2):
        rows = pl.ds(i * SUB, SUB)
        near = pl.ds(2 * i * SUB, SUB)
        far = strip(lax.rem(turn() + 2 * i + count, count))
        keep[rows, :] = held[near, :] + came[near, :]
        send[rows, :] = held[far, :] + came[far, :]


def group_kernel(held_a, came_a, held_b, came_b, out):
    group = lax.axis_index("layer") // 4
    half = held_a.shape[1]
    for i in range(4):
        source, target = pl.ds(i * SUB, SUB), strip(lax.rem(group + i, 4))
        out[target, :half] = held_a[source, :] + came_a[source, :]
        out[target, half:] = held_b[source, :] + came_b[source, :]


def last_kernel(came, out):
    x = lax.axis_index("row") // 2
    for index, t in enumerate(ORDER):
        source = pl.ds(index * 2 * TILE, 2 * TILE)
        target = pl.ds(pl.multiple_of(lax.rem(x + t, N_X) * 2 * TILE, 2 * TILE), 2 * TILE)
        a, b, c, d = (came[pl.ds(i * SUB, SUB), source] for i in range(4))
        out[:, target] = (a + b) + (c + d)


def swap(value):
    return lax.ppermute(value, "row", [(i, i ^ 1) for i in range(N_ROW)])


def fetch(value, t):
    pairs = []
    for x in range(N_X):
        for y in range(N_COL):
            pairs.append(((2 * x) * N_COL + (y + t) % N_COL, (2 * x) * N_COL + y))
            pairs.append(((2 * ((x + t) % N_X) + 1) * N_COL + y, (2 * x + 1) * N_COL + y))
    return lax.ppermute(value, ("row", "col"), pairs)


def pass_on(value, distance):
    pairs = []
    for z in range(N_LAYER):
        for row in range(N_ROW):
            to = (z + (distance if row % 2 == 0 else -distance)) % N_LAYER
            pairs.append((z * N_ROW + row, to * N_ROW + row))
    return lax.ppermute(value, ("layer", "row"), pairs)


def on_device(graph, pattern):
    inner = graph.shape[0]
    (masked,) = call(mask_kernel, [(inner, TILE)], (graph, pattern.reshape(-1)), [VMEM, SMEM])
    (pair,) = call(pair_kernel, [(2 * inner, TILE)], (masked, swap(masked)))
    came = {t: fetch(pair, t) for t in (1, 3)}
    far = (fetch(came[1][:inner], 1), fetch(came[3][inner:], 3))
    swapped = {t: swap(came[t]) for t in (1, 3)}
    known, wide = 3 * TILE, 6 * TILE
    parts = call(
        first_product_kernel,
        [((known, inner), BF16)] * 2 + [((inner, wide), BF16)] * 2 + [(known, wide)],
        (pair, came[1], swapped[1], came[3], swapped[3]),
        flops=6 * known * wide * inner,
        nbytes=8 << 20,
    )
    (last,) = call(join_kernel, [(2 * inner, TILE)], far)
    split_scratch = [pltpu.VMEM((TILE, inner), BF16)] * 2 + [pltpu.VMEM((inner, 2 * TILE), BF16)] * 2
    made = call(
        second_product_kernel,
        [(8 * SUB, 4 * TILE)] * 4,
        (last, swap(last), *parts),
        scratch=split_scratch + [pltpu.VMEM((4 * TILE, 8 * TILE), F32)],
        flops=6 * 7 * TILE * 2 * TILE * inner,
        nbytes=8 << 20,
    )
    sends, keeps = list(made[:2]), list(made[2:])
    arrived = [pass_on(sends[half], 1) for half in range(2)]
    for half in range(2):
        sends[half], keeps[half] = call(
            stage_kernel, [(4 * SUB, 4 * TILE)] * 2, (keeps[half], arrived[half])
        )
        arrived[half] = pass_on(sends[half], 2)
    (chunks,) = call(
        group_kernel, [(4 * SUB, 8 * TILE)], (keeps[0], arrived[0], keeps[1], arrived[1])
    )
    groups = [[4 * g + s for g in range(4)] for s in range(4)]
    came = lax.all_to_all(chunks, "layer", 0, 0, tiled=True, axis_index_groups=groups)
    return call(last_kernel, [(SUB, 8 * TILE)], (came,))[0]


def solution(mesh):
    placed = (P("layer", ("row", "col")), P("layer", ("row", "col")))
    return jax.shard_map(
        on_device, mesh=mesh, in_specs=placed, out_specs=P(("row", "layer"), "col"), check_vma=False
    )
```

```python
import functools

import jax
import jax.numpy as jnp
from jax import lax
from jax.experimental import pallas as pl
from jax.experimental.pallas import tpu as pltpu
from jax.sharding import PartitionSpec as P

TILE = 128
N_LAYER = 16
N_X = 4
N_ROW = 8
N_COL = 4
SUB = 32
ORDER = (0, 1, 3, 2)
VMEM = pl.BlockSpec(memory_space=pltpu.VMEM)
SMEM = pl.BlockSpec(memory_space=pltpu.SMEM)
LIMIT = 40 * 1024 * 1024
F32, BF16 = jnp.float32, jnp.bfloat16


def call(kernel, outs, operands, specs=None, scratch=(), flops=0, nbytes=1 << 20):
    outs = [o if isinstance(o[0], tuple) else (o, F32) for o in outs]
    return pl.pallas_call(
        kernel,
        out_shape=tuple(jax.ShapeDtypeStruct(s, d) for s, d in outs),
        in_specs=specs or [VMEM] * len(operands),
        out_specs=tuple(VMEM for _ in outs),
        scratch_shapes=list(scratch),
        compiler_params=pltpu.CompilerParams(vmem_limit_bytes=LIMIT),
        cost_estimate=pl.CostEstimate(flops=flops, bytes_accessed=nbytes, transcendentals=0),
    )(*operands)


def mask_kernel(graph, pattern, masked):
    for k in range(graph.shape[0] // TILE):
        rows = pl.ds(k * TILE, TILE)
        masked[rows, :] = graph[rows, :] * pattern[k].astype(F32)


def core():
    return lax.rem(lax.axis_index("row"), 2)


def join_kernel(first, second, pair):
    inner = first.shape[0]
    pair[:inner, :] = first[...]
    pair[inner:, :] = second[...]


def split(value):
    high = value.astype(BF16)
    low = (value - high.astype(F32)).astype(BF16)
    return high, low


dot = functools.partial(jnp.dot, preferred_element_type=F32)


def product(left_high, left_low, right_high, right_low):
    return dot(left_high, right_high) + (dot(left_high, right_low) + dot(left_low, right_high))


def take_left(index, block, left_high, left_low):
    rows = pl.ds(index * TILE, TILE)
    high, low = split(block[...].T)
    left_high[rows, :] = high
    left_low[rows, :] = low


def take_right(index, parity, block, right_high, right_low):
    start = 2 * index * TILE + parity * TILE
    columns = pl.ds(start if isinstance(start, int) else pl.multiple_of(start, TILE), TILE)
    high, low = split(block[...])
    right_high[:, columns] = high
    right_low[:, columns] = low


def place(index, first, second, first_swapped, second_swapped, left, right):
    @pl.when(core() == 0)
    def _():
        take_left(index, first, *left)
        take_right(index, 0, second_swapped, *right)
        take_right(index, 1, first_swapped, *right)

    @pl.when(core() == 1)
    def _():
        take_left(index, second_swapped, *left)
        take_right(index, 0, second, *right)
        take_right(index, 1, first, *right)


def halves(pair):
    inner = pair.shape[0] // 2
    return pair.at[pl.ds(0, inner), :], pair.at[pl.ds(inner, inner), :]


def first_product_kernel(own, other, o1, s1, o3, s3, oo, ss, left_high, left_low, right_high, right_low, total):
    left, right = (left_high, left_low), (right_high, right_low)
    take_left(0, own, *left)
    take_right(0, core(), own, *right)
    take_right(0, 1 - core(), other, *right)
    (o1_swapped, o3_swapped), (s1_swapped, s3_swapped) = halves(oo), halves(ss)
    place(1, o1, s1, o1_swapped, s1_swapped, left, right)
    place(2, o3, s3, o3_swapped, s3_swapped, left, right)
    for index in range(3):
        columns = pl.ds(index * 2 * TILE, 2 * TILE)
        total[:, columns] = product(left_high[...], left_low[...], right_high[:, columns], right_low[:, columns])


def turn():
    return 1 - 2 * core()


def strip(index):
    return pl.ds(pl.multiple_of(index * SUB, SUB), SUB)


def second_product_kernel(o2, s2, both, left_high, left_low, right_high, right_low, part, *refs):
    sends, keeps = refs[0:2], refs[2:4]
    last_high, last_low, far_high, far_low, total = refs[4:]
    z, y = lax.axis_index("layer"), lax.axis_index("col")
    place(0, o2, s2, *halves(both), (last_high, last_low), (far_high, far_low))
    known = part.shape[0]
    total[:known, : part.shape[1]] = part[...]
    total[known:, : part.shape[1]] = product(last_high[...], last_low[...], right_high[...], right_low[...])
    columns = pl.ds(part.shape[1], 2 * TILE)
    total[:known, columns] = product(left_high[...], left_low[...], far_high[...], far_low[...])
    total[known:, columns] = product(last_high[...], last_low[...], far_high[...], far_low[...])

    def rows_of(layer):
        t = lax.rem(layer // 4 - y + N_COL, N_COL)
        index = jnp.where(t < 2, t, 5 - t)
        return strip(index * 4 + lax.rem(layer, 4))

    for j in range(N_LAYER // 2):
        keep = rows_of(lax.rem(z + 2 * j, N_LAYER))
        send = rows_of(lax.rem(z + turn() + 2 * j + N_LAYER, N_LAYER))
        rows = pl.ds(j * SUB, SUB)
        for half in range(2):
            columns = pl.ds(half * 4 * TILE, 4 * TILE)
            keeps[half][rows, :] = total[keep, columns]
            sends[half][rows, :] = total[send, columns]


def stage_kernel(held, came, send, keep):
    count = held.shape[0] // SUB
    for i in range(count // 2):
        rows = pl.ds(i * SUB, SUB)
        near = pl.ds(2 * i * SUB, SUB)
        far = strip(lax.rem(turn() + 2 * i + count, count))
        keep[rows, :] = held[near, :] + came[near, :]
        send[rows, :] = held[far, :] + came[far, :]


def last_kernel(held_a, came_a, held_b, came_b, out):
    x = lax.axis_index("row") // 2
    for index, t in enumerate(ORDER):
        held, came = ((held_a, came_a), (held_b, came_b))[index // 2]
        source = pl.ds((index % 2) * 2 * TILE, 2 * TILE)
        target = pl.ds(pl.multiple_of(lax.rem(x + t, N_X) * 2 * TILE, 2 * TILE), 2 * TILE)
        out[:, target] = held[:, source] + came[:, source]


def swap(value):
    return lax.ppermute(value, "row", [(i, i ^ 1) for i in range(N_ROW)])


def fetch(value, t):
    pairs = []
    for x in range(N_X):
        for y in range(N_COL):
            pairs.append(((2 * x) * N_COL + (y + t) % N_COL, (2 * x) * N_COL + y))
            pairs.append(((2 * ((x + t) % N_X) + 1) * N_COL + y, (2 * x + 1) * N_COL + y))
    return lax.ppermute(value, ("row", "col"), pairs)


def pass_on(value, distance):
    pairs = []
    for z in range(N_LAYER):
        for row in range(N_ROW):
            to = (z + (distance if row % 2 == 0 else -distance)) % N_LAYER
            pairs.append((z * N_ROW + row, to * N_ROW + row))
    return lax.ppermute(value, ("layer", "row"), pairs)


def on_device(graph, pattern):
    inner = graph.shape[0]
    (masked,) = call(mask_kernel, [(inner, TILE)], (graph, pattern.reshape(-1)), [VMEM, SMEM])
    other = swap(masked)
    o1, o3 = fetch(masked, 1), fetch(masked, 3)
    s3, s1 = fetch(other, 3), fetch(other, 1)
    o2, s2 = fetch(o1, 1), fetch(s3, 3)

    def swap_two(first, second):
        return swap(call(join_kernel, [(2 * inner, TILE)], (first, second))[0])

    known, wide = 3 * TILE, 6 * TILE
    parts = call(
        first_product_kernel,
        [((known, inner), BF16)] * 2 + [((inner, wide), BF16)] * 2 + [(known, wide)],
        (masked, other, o1, s1, o3, s3, swap_two(o1, o3), swap_two(s1, s3)),
        flops=6 * known * wide * inner,
        nbytes=8 << 20,
    )
    split_scratch = [pltpu.VMEM((TILE, inner), BF16)] * 2 + [pltpu.VMEM((inner, 2 * TILE), BF16)] * 2
    made = call(
        second_product_kernel,
        [(8 * SUB, 4 * TILE)] * 4,
        (o2, s2, swap_two(o2, s2), *parts),
        scratch=split_scratch + [pltpu.VMEM((4 * TILE, 8 * TILE), F32)],
        flops=6 * 7 * TILE * 2 * TILE * inner,
        nbytes=8 << 20,
    )
    sends, keeps = list(made[:2]), list(made[2:])
    arrived = [pass_on(sends[half], 1) for half in range(2)]
    for stage in (1, 2, 3):
        count = 8 >> stage
        for half in range(2):
            sends[half], keeps[half] = call(
                stage_kernel, [(count * SUB, 4 * TILE)] * 2, (keeps[half], arrived[half])
            )
            arrived[half] = pass_on(sends[half], 1 << stage)
    return call(last_kernel, [(SUB, 8 * TILE)], (keeps[0], arrived[0], keeps[1], arrived[1]))[0]


def solution(mesh):
    placed = (P("layer", ("row", "col")), P("layer", ("row", "col")))
    return jax.shard_map(
        on_device, mesh=mesh, in_specs=placed, out_specs=P(("row", "layer"), "col"), check_vma=False
    )
```

```python
import functools

import jax
import jax.numpy as jnp
from jax import lax
from jax.experimental import pallas as pl
from jax.experimental.pallas import tpu as pltpu
from jax.sharding import PartitionSpec as P

TILE = 128
N_LAYER = 16
N_X = 4
N_ROW = 8
N_COL = 4
SUB = 32
ORDER = (0, 1, 3, 2)
VMEM = pl.BlockSpec(memory_space=pltpu.VMEM)
SMEM = pl.BlockSpec(memory_space=pltpu.SMEM)
LIMIT = 40 * 1024 * 1024
F32, BF16 = jnp.float32, jnp.bfloat16


def call(kernel, outs, operands, specs=None, scratch=(), flops=0, nbytes=1 << 20):
    outs = [o if isinstance(o[0], tuple) else (o, F32) for o in outs]
    return pl.pallas_call(
        kernel,
        out_shape=tuple(jax.ShapeDtypeStruct(s, d) for s, d in outs),
        in_specs=specs or [VMEM] * len(operands),
        out_specs=tuple(VMEM for _ in outs),
        scratch_shapes=list(scratch),
        compiler_params=pltpu.CompilerParams(vmem_limit_bytes=LIMIT),
        cost_estimate=pl.CostEstimate(flops=flops, bytes_accessed=nbytes, transcendentals=0),
    )(*operands)


def mask_kernel(graph, pattern, masked):
    for k in range(graph.shape[0] // TILE):
        rows = pl.ds(k * TILE, TILE)
        masked[rows, :] = graph[rows, :] * pattern[k].astype(F32)


def core():
    return lax.rem(lax.axis_index("row"), 2)


def join_kernel(first, second, pair):
    inner = first.shape[0]
    pair[:inner, :] = first[...]
    pair[inner:, :] = second[...]


def split(value):
    high = value.astype(BF16)
    low = (value - high.astype(F32)).astype(BF16)
    return high, low


dot = functools.partial(jnp.dot, preferred_element_type=F32)


def product(left_high, left_low, right_high, right_low):
    return dot(left_high, right_high) + (dot(left_high, right_low) + dot(left_low, right_high))


def take_left(index, block, left_high, left_low):
    rows = pl.ds(index * TILE, TILE)
    high, low = split(block[...].T)
    left_high[rows, :] = high
    left_low[rows, :] = low


def take_right(index, parity, block, right_high, right_low):
    start = 2 * index * TILE + parity * TILE
    columns = pl.ds(start if isinstance(start, int) else pl.multiple_of(start, TILE), TILE)
    high, low = split(block[...])
    right_high[:, columns] = high
    right_low[:, columns] = low


def place(index, first, second, first_swapped, second_swapped, left, right):
    @pl.when(core() == 0)
    def _():
        take_left(index, first, *left)
        take_right(index, 0, second_swapped, *right)
        take_right(index, 1, first_swapped, *right)

    @pl.when(core() == 1)
    def _():
        take_left(index, second_swapped, *left)
        take_right(index, 0, second, *right)
        take_right(index, 1, first, *right)


def halves(pair):
    inner = pair.shape[0] // 2
    return pair.at[pl.ds(0, inner), :], pair.at[pl.ds(inner, inner), :]


def first_product_kernel(own, other, o1, s1, o3, s3, oo, ss, left_high, left_low, right_high, right_low, total):
    left, right = (left_high, left_low), (right_high, right_low)
    take_left(0, own, *left)
    take_right(0, core(), own, *right)
    take_right(0, 1 - core(), other, *right)
    (o1_swapped, o3_swapped), (s1_swapped, s3_swapped) = halves(oo), halves(ss)
    place(1, o1, s1, o1_swapped, s1_swapped, left, right)
    place(2, o3, s3, o3_swapped, s3_swapped, left, right)
    for index in range(3):
        columns = pl.ds(index * 2 * TILE, 2 * TILE)
        total[:, columns] = product(left_high[...], left_low[...], right_high[:, columns], right_low[:, columns])


def turn():
    return 1 - 2 * core()


def strip(index):
    return pl.ds(pl.multiple_of(index * SUB, SUB), SUB)


def second_product_kernel(o2, s2, both, left_high, left_low, right_high, right_low, part, *refs):
    sends, keeps = refs[0:2], refs[2:4]
    last_high, last_low, far_high, far_low, total = refs[4:]
    z, y = lax.axis_index("layer"), lax.axis_index("col")
    place(0, o2, s2, *halves(both), (last_high, last_low), (far_high, far_low))
    known = part.shape[0]
    total[:known, : part.shape[1]] = part[...]
    total[known:, : part.shape[1]] = product(last_high[...], last_low[...], right_high[...], right_low[...])
    columns = pl.ds(part.shape[1], 2 * TILE)
    total[:known, columns] = product(left_high[...], left_low[...], far_high[...], far_low[...])
    total[known:, columns] = product(last_high[...], last_low[...], far_high[...], far_low[...])

    def rows_of(layer):
        t = lax.rem(layer // 4 - y + N_COL, N_COL)
        index = jnp.where(t < 2, t, 5 - t)
        return strip(index * 4 + lax.rem(layer, 4))

    for j in range(N_LAYER // 2):
        keep = rows_of(lax.rem(z + 2 * j, N_LAYER))
        send = rows_of(lax.rem(z + turn() + 2 * j + N_LAYER, N_LAYER))
        rows = pl.ds(j * SUB, SUB)
        for half in range(2):
            columns = pl.ds(half * 4 * TILE, 4 * TILE)
            keeps[half][rows, :] = total[keep, columns]
            sends[half][rows, :] = total[send, columns]


def stage_kernel(held, came, send, keep):
    count = held.shape[0] // SUB
    for i in range(count // 2):
        rows = pl.ds(i * SUB, SUB)
        near = pl.ds(2 * i * SUB, SUB)
        far = strip(lax.rem(turn() + 2 * i + count, count))
        keep[rows, :] = held[near, :] + came[near, :]
        send[rows, :] = held[far, :] + came[far, :]


def group_kernel(held, came, own, up, far, down):
    for i, out in enumerate((own, up, far, down)):
        rows = pl.ds(i * SUB, SUB)
        out[...] = held[rows, :] + came[rows, :]


def up_kernel(first, second, came, out):
    half = first.shape[1]
    out[:, :half] = first[...] + came[...]
    out[:, half:] = second[...]


def down_kernel(first, second, came, out):
    half = first.shape[1]
    out[:, :half] = first[...]
    out[:, half:] = second[...] + came[...]


def last_kernel(first, second, from_below, from_above, out):
    x = lax.axis_index("row") // 2
    for index, t in enumerate(ORDER):
        source = pl.ds(index * 2 * TILE, 2 * TILE)
        own = (first, second)[index // 2][:, pl.ds((index % 2) * 2 * TILE, 2 * TILE)]
        target = pl.ds(pl.multiple_of(lax.rem(x + t, N_X) * 2 * TILE, 2 * TILE), 2 * TILE)
        out[:, target] = own + (from_below[:, source] + from_above[:, source])


def swap(value):
    return lax.ppermute(value, "row", [(i, i ^ 1) for i in range(N_ROW)])


def fetch(value, t):
    pairs = []
    for x in range(N_X):
        for y in range(N_COL):
            pairs.append(((2 * x) * N_COL + (y + t) % N_COL, (2 * x) * N_COL + y))
            pairs.append(((2 * ((x + t) % N_X) + 1) * N_COL + y, (2 * x + 1) * N_COL + y))
    return lax.ppermute(value, ("row", "col"), pairs)


def pass_on(value, distance):
    pairs = []
    for z in range(N_LAYER):
        for row in range(N_ROW):
            to = (z + (distance if row % 2 == 0 else -distance)) % N_LAYER
            pairs.append((z * N_ROW + row, to * N_ROW + row))
    return lax.ppermute(value, ("layer", "row"), pairs)


def shift_layers(value, distance):
    return lax.ppermute(value, "layer", [(z, (z + distance) % N_LAYER) for z in range(N_LAYER)])


def on_device(graph, pattern):
    inner = graph.shape[0]
    (masked,) = call(mask_kernel, [(inner, TILE)], (graph, pattern.reshape(-1)), [VMEM, SMEM])
    other = swap(masked)
    o1, o3 = fetch(masked, 1), fetch(masked, 3)
    s3, s1 = fetch(other, 3), fetch(other, 1)
    o2, s2 = fetch(o1, 1), fetch(s3, 3)

    def swap_two(first, second):
        return swap(call(join_kernel, [(2 * inner, TILE)], (first, second))[0])

    known, wide = 3 * TILE, 6 * TILE
    parts = call(
        first_product_kernel,
        [((known, inner), BF16)] * 2 + [((inner, wide), BF16)] * 2 + [(known, wide)],
        (masked, other, o1, s1, o3, s3, swap_two(o1, o3), swap_two(s1, s3)),
        flops=6 * known * wide * inner,
        nbytes=8 << 20,
    )
    split_scratch = [pltpu.VMEM((TILE, inner), BF16)] * 2 + [pltpu.VMEM((inner, 2 * TILE), BF16)] * 2
    made = call(
        second_product_kernel,
        [(8 * SUB, 4 * TILE)] * 4,
        (o2, s2, swap_two(o2, s2), *parts),
        scratch=split_scratch + [pltpu.VMEM((4 * TILE, 8 * TILE), F32)],
        flops=6 * 7 * TILE * 2 * TILE * inner,
        nbytes=8 << 20,
    )
    sends, keeps = list(made[:2]), list(made[2:])
    arrived = [pass_on(sends[half], 1) for half in range(2)]
    for half in range(2):
        sends[half], keeps[half] = call(
            stage_kernel, [(4 * SUB, 4 * TILE)] * 2, (keeps[half], arrived[half])
        )
        arrived[half] = pass_on(sends[half], 2)
    first, second = (
        call(group_kernel, [(SUB, 4 * TILE)] * 4, (keeps[half], arrived[half])) for half in range(2)
    )
    chunk = [(SUB, 8 * TILE)]
    (up,) = call(up_kernel, chunk, (first[1], second[1], shift_layers(first[2], 4)))
    (down,) = call(down_kernel, chunk, (first[3], second[3], shift_layers(second[2], -4)))
    ends = (first[0], second[0], shift_layers(up, 4), shift_layers(down, -4))
    return call(last_kernel, chunk, ends)[0]


def solution(mesh):
    placed = (P("layer", ("row", "col")), P("layer", ("row", "col")))
    return jax.shard_map(
        on_device, mesh=mesh, in_specs=placed, out_specs=P(("row", "layer"), "col"), check_vma=False
    )
```

```python
import functools

import jax
import jax.numpy as jnp
from jax import lax
from jax.experimental import pallas as pl
from jax.experimental.pallas import tpu as pltpu
from jax.sharding import PartitionSpec as P

TILE = 128
N_LAYER = 16
N_X = 4
N_ROW = 8
N_COL = 4
SUB = 32
ORDER = (0, 1, 3, 2)
VMEM = pl.BlockSpec(memory_space=pltpu.VMEM)
SMEM = pl.BlockSpec(memory_space=pltpu.SMEM)
LIMIT = 40 * 1024 * 1024
F32, BF16 = jnp.float32, jnp.bfloat16


def call(kernel, outs, operands, specs=None, scratch=(), flops=0, nbytes=1 << 20):
    outs = [o if isinstance(o[0], tuple) else (o, F32) for o in outs]
    return pl.pallas_call(
        kernel,
        out_shape=tuple(jax.ShapeDtypeStruct(s, d) for s, d in outs),
        in_specs=specs or [VMEM] * len(operands),
        out_specs=tuple(VMEM for _ in outs),
        scratch_shapes=list(scratch),
        compiler_params=pltpu.CompilerParams(vmem_limit_bytes=LIMIT),
        cost_estimate=pl.CostEstimate(flops=flops, bytes_accessed=nbytes, transcendentals=0),
    )(*operands)


def mask_kernel(graph, pattern, masked):
    for k in range(graph.shape[0] // TILE):
        rows = pl.ds(k * TILE, TILE)
        masked[rows, :] = graph[rows, :] * pattern[k].astype(F32)


def core():
    return lax.rem(lax.axis_index("row"), 2)


def join_kernel(first, second, pair):
    inner = first.shape[0]
    pair[:inner, :] = first[...]
    pair[inner:, :] = second[...]


def split(value):
    high = value.astype(BF16)
    low = (value - high.astype(F32)).astype(BF16)
    return high, low


dot = functools.partial(jnp.dot, preferred_element_type=F32)


def product(left_high, left_low, right_high, right_low):
    return dot(left_high, right_high) + (dot(left_high, right_low) + dot(left_low, right_high))


def take_left(index, block, left_high, left_low):
    rows = pl.ds(index * TILE, TILE)
    high, low = split(block[...].T)
    left_high[rows, :] = high
    left_low[rows, :] = low


def take_right(index, parity, block, right_high, right_low):
    start = 2 * index * TILE + parity * TILE
    columns = pl.ds(start if isinstance(start, int) else pl.multiple_of(start, TILE), TILE)
    high, low = split(block[...])
    right_high[:, columns] = high
    right_low[:, columns] = low


def place(index, first, second, first_swapped, second_swapped, left, right):
    @pl.when(core() == 0)
    def _():
        take_left(index, first, *left)
        take_right(index, 0, second_swapped, *right)
        take_right(index, 1, first_swapped, *right)

    @pl.when(core() == 1)
    def _():
        take_left(index, second_swapped, *left)
        take_right(index, 0, second, *right)
        take_right(index, 1, first, *right)


def halves(pair):
    inner = pair.shape[0] // 2
    return pair.at[pl.ds(0, inner), :], pair.at[pl.ds(inner, inner), :]


def first_product_kernel(own, other, o1, s1, o3, s3, oo, ss, left_high, left_low, right_high, right_low, total):
    left, right = (left_high, left_low), (right_high, right_low)
    take_left(0, own, *left)
    take_right(0, core(), own, *right)
    take_right(0, 1 - core(), other, *right)
    (o1_swapped, o3_swapped), (s1_swapped, s3_swapped) = halves(oo), halves(ss)
    place(1, o1, s1, o1_swapped, s1_swapped, left, right)
    place(2, o3, s3, o3_swapped, s3_swapped, left, right)
    for index in range(3):
        columns = pl.ds(index * 2 * TILE, 2 * TILE)
        total[:, columns] = product(left_high[...], left_low[...], right_high[:, columns], right_low[:, columns])


def turn():
    return 1 - 2 * core()


def strip(index):
    return pl.ds(pl.multiple_of(index * SUB, SUB), SUB)


def second_product_kernel(o2, s2, both, left_high, left_low, right_high, right_low, part, *refs):
    sends, keeps = refs[0:2], refs[2:4]
    last_high, last_low, far_high, far_low, total = refs[4:]
    z, y = lax.axis_index("layer"), lax.axis_index("col")
    place(0, o2, s2, *halves(both), (last_high, last_low), (far_high, far_low))
    known = part.shape[0]
    total[:known, : part.shape[1]] = part[...]
    total[known:, : part.shape[1]] = product(last_high[...], last_low[...], right_high[...], right_low[...])
    columns = pl.ds(part.shape[1], 2 * TILE)
    total[:known, columns] = product(left_high[...], left_low[...], far_high[...], far_low[...])
    total[known:, columns] = product(last_high[...], last_low[...], far_high[...], far_low[...])

    def rows_of(layer):
        t = lax.rem(layer // 4 - y + N_COL, N_COL)
        index = jnp.where(t < 2, t, 5 - t)
        return strip(index * 4 + lax.rem(layer, 4))

    for j in range(N_LAYER // 2):
        keep = rows_of(lax.rem(z + 2 * j, N_LAYER))
        send = rows_of(lax.rem(z + turn() + 2 * j + N_LAYER, N_LAYER))
        rows = pl.ds(j * SUB, SUB)
        for half in range(2):
            columns = pl.ds(half * 4 * TILE, 4 * TILE)
            keeps[half][rows, :] = total[keep, columns]
            sends[half][rows, :] = total[send, columns]


def stage_kernel(held, came, send, keep):
    count = held.shape[0] // SUB
    for i in range(count // 2):
        rows = pl.ds(i * SUB, SUB)
        near = pl.ds(2 * i * SUB, SUB)
        far = strip(lax.rem(turn() + 2 * i + count, count))
        keep[rows, :] = held[near, :] + came[near, :]
        send[rows, :] = held[far, :] + came[far, :]


def group_kernel(held, came, own, up, far, down):
    for i, out in enumerate((own, up, far, down)):
        rows = pl.ds(i * SUB, SUB)
        out[...] = held[rows, :] + came[rows, :]


def add_kernel(held, came, out):
    out[...] = held[...] + came[...]


def last_kernel(*refs):
    halves_of, out = (refs[0:3], refs[3:6]), refs[6]
    x = lax.axis_index("row") // 2
    for index, t in enumerate(ORDER):
        source = pl.ds((index % 2) * 2 * TILE, 2 * TILE)
        target = pl.ds(pl.multiple_of(lax.rem(x + t, N_X) * 2 * TILE, 2 * TILE), 2 * TILE)
        own, below, above = halves_of[index // 2]
        out[:, target] = own[:, source] + (below[:, source] + above[:, source])


def swap(value):
    return lax.ppermute(value, "row", [(i, i ^ 1) for i in range(N_ROW)])


def fetch(value, t):
    pairs = []
    for x in range(N_X):
        for y in range(N_COL):
            pairs.append(((2 * x) * N_COL + (y + t) % N_COL, (2 * x) * N_COL + y))
            pairs.append(((2 * ((x + t) % N_X) + 1) * N_COL + y, (2 * x + 1) * N_COL + y))
    return lax.ppermute(value, ("row", "col"), pairs)


def pass_on(value, distance):
    pairs = []
    for z in range(N_LAYER):
        for row in range(N_ROW):
            to = (z + (distance if row % 2 == 0 else -distance)) % N_LAYER
            pairs.append((z * N_ROW + row, to * N_ROW + row))
    return lax.ppermute(value, ("layer", "row"), pairs)


def shift_layers(value, distance):
    return lax.ppermute(value, "layer", [(z, (z + distance) % N_LAYER) for z in range(N_LAYER)])


def on_device(graph, pattern):
    inner = graph.shape[0]
    (masked,) = call(mask_kernel, [(inner, TILE)], (graph, pattern.reshape(-1)), [VMEM, SMEM])
    other = swap(masked)
    o1, o3 = fetch(masked, 1), fetch(masked, 3)
    s3, s1 = fetch(other, 3), fetch(other, 1)
    o2, s2 = fetch(o1, 1), fetch(s3, 3)

    def swap_two(first, second):
        return swap(call(join_kernel, [(2 * inner, TILE)], (first, second))[0])

    known, wide = 3 * TILE, 6 * TILE
    parts = call(
        first_product_kernel,
        [((known, inner), BF16)] * 2 + [((inner, wide), BF16)] * 2 + [(known, wide)],
        (masked, other, o1, s1, o3, s3, swap_two(o1, o3), swap_two(s1, s3)),
        flops=6 * known * wide * inner,
        nbytes=8 << 20,
    )
    split_scratch = [pltpu.VMEM((TILE, inner), BF16)] * 2 + [pltpu.VMEM((inner, 2 * TILE), BF16)] * 2
    made = call(
        second_product_kernel,
        [(8 * SUB, 4 * TILE)] * 4,
        (o2, s2, swap_two(o2, s2), *parts),
        scratch=split_scratch + [pltpu.VMEM((4 * TILE, 8 * TILE), F32)],
        flops=6 * 7 * TILE * 2 * TILE * inner,
        nbytes=8 << 20,
    )
    sends, keeps = list(made[:2]), list(made[2:])
    arrived = [pass_on(sends[half], 1) for half in range(2)]
    for half in range(2):
        sends[half], keeps[half] = call(
            stage_kernel, [(4 * SUB, 4 * TILE)] * 2, (keeps[half], arrived[half])
        )
        arrived[half] = pass_on(sends[half], 2)
    first, second = (
        call(group_kernel, [(SUB, 4 * TILE)] * 4, (keeps[half], arrived[half])) for half in range(2)
    )
    piece = [(SUB, 4 * TILE)]
    relayed_up, relayed_down = shift_layers(first[2], 4), shift_layers(second[2], -4)
    first_above, second_below = shift_layers(first[3], -4), shift_layers(second[1], 4)
    first_below = shift_layers(call(add_kernel, piece, (first[1], relayed_up))[0], 4)
    second_above = shift_layers(call(add_kernel, piece, (second[3], relayed_down))[0], -4)
    ends = (first[0], first_below, first_above, second[0], second_below, second_above)
    return call(last_kernel, [(SUB, 8 * TILE)], ends)[0]


def solution(mesh):
    placed = (P("layer", ("row", "col")), P("layer", ("row", "col")))
    return jax.shard_map(
        on_device, mesh=mesh, in_specs=placed, out_specs=P(("row", "layer"), "col"), check_vma=False
    )
```

```python
import functools

import jax
import jax.numpy as jnp
from jax import lax
from jax.experimental import pallas as pl
from jax.experimental.pallas import tpu as pltpu
from jax.sharding import PartitionSpec as P

TILE = 128
N_LAYER = 16
N_X = 4
N_ROW = 8
N_COL = 4
SUB = 32
ORDER = (0, 1, 3, 2)
VMEM = pl.BlockSpec(memory_space=pltpu.VMEM)
SMEM = pl.BlockSpec(memory_space=pltpu.SMEM)
LIMIT = 40 * 1024 * 1024
F32, BF16 = jnp.float32, jnp.bfloat16


def call(kernel, outs, operands, specs=None, scratch=(), flops=0, nbytes=1 << 20, after=None):
    if after is not None:
        inner_kernel, count = kernel, len(operands)
        kernel = lambda *refs: inner_kernel(*refs[:count], *refs[count + 1 :])
        specs = [VMEM] * count + [pl.BlockSpec(memory_space=pl.ANY)]
        operands = (*operands, after)
    outs = [o if isinstance(o[0], tuple) else (o, F32) for o in outs]
    return pl.pallas_call(
        kernel,
        out_shape=tuple(jax.ShapeDtypeStruct(s, d) for s, d in outs),
        in_specs=specs or [VMEM] * len(operands),
        out_specs=tuple(VMEM for _ in outs),
        scratch_shapes=list(scratch),
        compiler_params=pltpu.CompilerParams(vmem_limit_bytes=LIMIT),
        cost_estimate=pl.CostEstimate(flops=flops, bytes_accessed=nbytes, transcendentals=0),
    )(*operands)


def mask_kernel(graph, pattern, masked):
    for k in range(graph.shape[0] // TILE):
        rows = pl.ds(k * TILE, TILE)
        masked[rows, :] = graph[rows, :] * pattern[k].astype(F32)


def core():
    return lax.rem(lax.axis_index("row"), 2)


def join_kernel(first, second, pair):
    inner = first.shape[0]
    pair[:inner, :] = first[...]
    pair[inner:, :] = second[...]


def split(value):
    high = value.astype(BF16)
    low = (value - high.astype(F32)).astype(BF16)
    return high, low


dot = functools.partial(jnp.dot, preferred_element_type=F32)


def product(left_high, left_low, right_high, right_low):
    return dot(left_high, right_high) + (dot(left_high, right_low) + dot(left_low, right_high))


def take_left(index, block, left_high, left_low):
    rows = pl.ds(index * TILE, TILE)
    high, low = split(block[...].T)
    left_high[rows, :] = high
    left_low[rows, :] = low


def take_right(index, parity, block, right_high, right_low):
    start = 2 * index * TILE + parity * TILE
    columns = pl.ds(start if isinstance(start, int) else pl.multiple_of(start, TILE), TILE)
    high, low = split(block[...])
    right_high[:, columns] = high
    right_low[:, columns] = low


def place(index, first, second, first_swapped, second_swapped, left, right):
    @pl.when(core() == 0)
    def _():
        take_left(index, first, *left)
        take_right(index, 0, second_swapped, *right)
        take_right(index, 1, first_swapped, *right)

    @pl.when(core() == 1)
    def _():
        take_left(index, second_swapped, *left)
        take_right(index, 0, second, *right)
        take_right(index, 1, first, *right)


def halves(pair):
    inner = pair.shape[0] // 2
    return pair.at[pl.ds(0, inner), :], pair.at[pl.ds(inner, inner), :]


def first_product_kernel(own, other, o1, s1, o3, s3, oo, ss, left_high, left_low, right_high, right_low, total):
    left, right = (left_high, left_low), (right_high, right_low)
    take_left(0, own, *left)
    take_right(0, core(), own, *right)
    take_right(0, 1 - core(), other, *right)
    (o1_swapped, o3_swapped), (s1_swapped, s3_swapped) = halves(oo), halves(ss)
    place(1, o1, s1, o1_swapped, s1_swapped, left, right)
    place(2, o3, s3, o3_swapped, s3_swapped, left, right)
    for index in range(3):
        columns = pl.ds(index * 2 * TILE, 2 * TILE)
        total[:, columns] = product(left_high[...], left_low[...], right_high[:, columns], right_low[:, columns])


def turn():
    return 1 - 2 * core()


def strip(index):
    return pl.ds(pl.multiple_of(index * SUB, SUB), SUB)


def scatter(total, send, keep):
    z, y = lax.axis_index("layer"), lax.axis_index("col")

    def rows_of(layer):
        t = lax.rem(layer // 4 - y + N_COL, N_COL)
        index = jnp.where(t < 2, t, 5 - t)
        return strip(index * 4 + lax.rem(layer, 4))

    for j in range(N_LAYER // 2):
        rows = pl.ds(j * SUB, SUB)
        keep[rows, :] = total[rows_of(lax.rem(z + 2 * j, N_LAYER)), :]
        send[rows, :] = total[rows_of(lax.rem(z + turn() + 2 * j + N_LAYER, N_LAYER)), :]


def second_product_kernel(o2, s2, both, right_high, right_low, part, send, keep, last_high, last_low, total):
    swapped = both.at[pl.ds(s2.shape[0], s2.shape[0]), :]

    @pl.when(core() == 0)
    def _():
        take_left(0, o2, last_high, last_low)

    @pl.when(core() == 1)
    def _():
        take_left(0, swapped, last_high, last_low)

    known, columns = part.shape[0], pl.ds(0, total.shape[1])
    total[:known, :] = part[:, columns]
    total[known:, :] = product(last_high[...], last_low[...], right_high[:, columns], right_low[:, columns])
    scatter(total, send, keep)


def third_product_kernel(o2, s2, both, last_high, last_low, left_high, left_low, right_high, right_low, part, *refs):
    send, keep, far_high, far_low, total = refs
    o2_swapped, s2_swapped = halves(both)

    @pl.when(core() == 0)
    def _():
        take_right(0, 0, s2_swapped, far_high, far_low)
        take_right(0, 1, o2_swapped, far_high, far_low)

    @pl.when(core() == 1)
    def _():
        take_right(0, 0, s2, far_high, far_low)
        take_right(0, 1, o2, far_high, far_low)

    known, wide = part.shape[0], 2 * TILE
    columns = pl.ds(part.shape[1] - wide, wide)
    total[:known, :wide] = part[:, columns]
    total[known:, :wide] = product(last_high[...], last_low[...], right_high[:, columns], right_low[:, columns])
    total[:known, wide:] = product(left_high[...], left_low[...], far_high[...], far_low[...])
    total[known:, wide:] = product(last_high[...], last_low[...], far_high[...], far_low[...])
    scatter(total, send, keep)


def stage_kernel(held, came, send, keep):
    count = held.shape[0] // SUB
    for i in range(count // 2):
        rows = pl.ds(i * SUB, SUB)
        near = pl.ds(2 * i * SUB, SUB)
        far = strip(lax.rem(turn() + 2 * i + count, count))
        keep[rows, :] = held[near, :] + came[near, :]
        send[rows, :] = held[far, :] + came[far, :]


def group_kernel(held, came, own, up, far, down):
    for i, out in enumerate((own, up, far, down)):
        rows = pl.ds(i * SUB, SUB)
        out[...] = held[rows, :] + came[rows, :]


def up_kernel(first, second, came, out):
    half = first.shape[1]
    out[:, :half] = first[...] + came[...]
    out[:, half:] = second[...]


def down_kernel(first, second, came, out):
    half = first.shape[1]
    out[:, :half] = first[...]
    out[:, half:] = second[...] + came[...]


def below_kernel(first, second, from_below, out):
    half = first.shape[1]
    out[:, :half] = first[...] + from_below[:, :half]
    out[:, half:] = second[...] + from_below[:, half:]


def last_kernel(held, from_above, out):
    x = lax.axis_index("row") // 2
    for index, t in enumerate(ORDER):
        source = pl.ds(index * 2 * TILE, 2 * TILE)
        target = pl.ds(pl.multiple_of(lax.rem(x + t, N_X) * 2 * TILE, 2 * TILE), 2 * TILE)
        out[:, target] = held[:, source] + from_above[:, source]


def swap(value):
    return lax.ppermute(value, "row", [(i, i ^ 1) for i in range(N_ROW)])


def fetch(value, t):
    pairs = []
    for x in range(N_X):
        for y in range(N_COL):
            pairs.append(((2 * x) * N_COL + (y + t) % N_COL, (2 * x) * N_COL + y))
            pairs.append(((2 * ((x + t) % N_X) + 1) * N_COL + y, (2 * x + 1) * N_COL + y))
    return lax.ppermute(value, ("row", "col"), pairs)


def pass_on(value, distance):
    pairs = []
    for z in range(N_LAYER):
        for row in range(N_ROW):
            to = (z + (distance if row % 2 == 0 else -distance)) % N_LAYER
            pairs.append((z * N_ROW + row, to * N_ROW + row))
    return lax.ppermute(value, ("layer", "row"), pairs)


def shift_layers(value, distance):
    return lax.ppermute(value, "layer", [(z, (z + distance) % N_LAYER) for z in range(N_LAYER)])


def on_device(graph, pattern):
    inner = graph.shape[0]
    (masked,) = call(mask_kernel, [(inner, TILE)], (graph, pattern.reshape(-1)), [VMEM, SMEM])
    other = swap(masked)
    o1, o3 = fetch(masked, 1), fetch(masked, 3)
    s3, s1 = fetch(other, 3), fetch(other, 1)
    o2, s2 = fetch(o1, 1), fetch(s3, 3)

    def swap_two(first, second):
        return swap(call(join_kernel, [(2 * inner, TILE)], (first, second))[0])

    known, wide = 3 * TILE, 6 * TILE
    parts = call(
        first_product_kernel,
        [((known, inner), BF16)] * 2 + [((inner, wide), BF16)] * 2 + [(known, wide)],
        (masked, other, o1, s1, o3, s3, swap_two(o1, o3), swap_two(s1, s3)),
        flops=6 * known * wide * inner,
        nbytes=8 << 20,
    )
    left_high, left_low, right_high, right_low, part = parts
    second = (o2, s2, swap_two(o2, s2))
    out = (8 * SUB, 4 * TILE)
    total = pltpu.VMEM((4 * TILE, 4 * TILE), F32)
    send_a, keep_a, *last = call(
        second_product_kernel,
        [out, out, ((TILE, inner), BF16), ((TILE, inner), BF16)],
        (*second, right_high, right_low, part),
        scratch=[total],
        flops=6 * TILE * 4 * TILE * inner,
        nbytes=4 << 20,
    )
    send_b, keep_b = call(
        third_product_kernel,
        [out, out],
        (*second, *last, left_high, left_low, right_high, right_low, part),
        scratch=[pltpu.VMEM((inner, 2 * TILE), BF16)] * 2 + [total],
        flops=6 * 5 * TILE * 2 * TILE * inner,
        nbytes=4 << 20,
    )
    sends, keeps = [send_a, send_b], [keep_a, keep_b]
    arrived = [pass_on(sends[half], 1) for half in range(2)]
    done = None
    for half in range(2):
        sends[half], keeps[half] = call(
            stage_kernel, [(4 * SUB, 4 * TILE)] * 2, (keeps[half], arrived[half]), after=done
        )
        done = keeps[half]
        arrived[half] = pass_on(sends[half], 2)
    first = call(group_kernel, [(SUB, 4 * TILE)] * 4, (keeps[0], arrived[0]))
    second = call(group_kernel, [(SUB, 4 * TILE)] * 4, (keeps[1], arrived[1]), after=first[0])
    chunk = [(SUB, 8 * TILE)]
    (up,) = call(up_kernel, chunk, (first[1], second[1], shift_layers(first[2], 4)))
    (down,) = call(down_kernel, chunk, (first[3], second[3], shift_layers(second[2], -4)), after=up)
    (held,) = call(below_kernel, chunk, (first[0], second[0], shift_layers(up, 4)))
    return call(last_kernel, chunk, (held, shift_layers(down, -4)))[0]


def solution(mesh):
    placed = (P("layer", ("row", "col")), P("layer", ("row", "col")))
    return jax.shard_map(
        on_device, mesh=mesh, in_specs=placed, out_specs=P(("row", "layer"), "col"), check_vma=False
    )
```

```python
import functools

import jax
import jax.numpy as jnp
from jax import lax
from jax.experimental import pallas as pl
from jax.experimental.pallas import tpu as pltpu
from jax.sharding import PartitionSpec as P

TILE = 128
N_LAYER = 16
N_X = 4
N_ROW = 8
N_COL = 4
SUB = 32
ORDER = (0, 1, 3, 2)
VMEM = pl.BlockSpec(memory_space=pltpu.VMEM)
SMEM = pl.BlockSpec(memory_space=pltpu.SMEM)
LIMIT = 40 * 1024 * 1024
F32, BF16 = jnp.float32, jnp.bfloat16


def call(kernel, outs, operands, specs=None, scratch=(), flops=0, nbytes=1 << 20, after=None):
    if after is not None:
        inner_kernel, count = kernel, len(operands)
        kernel = lambda *refs: inner_kernel(*refs[:count], *refs[count + 1 :])
        specs = [VMEM] * count + [pl.BlockSpec(memory_space=pl.ANY)]
        operands = (*operands, after)
    outs = [o if isinstance(o[0], tuple) else (o, F32) for o in outs]
    return pl.pallas_call(
        kernel,
        out_shape=tuple(jax.ShapeDtypeStruct(s, d) for s, d in outs),
        in_specs=specs or [VMEM] * len(operands),
        out_specs=tuple(VMEM for _ in outs),
        scratch_shapes=list(scratch),
        compiler_params=pltpu.CompilerParams(vmem_limit_bytes=LIMIT),
        cost_estimate=pl.CostEstimate(flops=flops, bytes_accessed=nbytes, transcendentals=0),
    )(*operands)


def mask_kernel(graph, pattern, masked):
    for k in range(graph.shape[0] // TILE):
        rows = pl.ds(k * TILE, TILE)
        masked[rows, :] = graph[rows, :] * pattern[k].astype(F32)


def core():
    return lax.rem(lax.axis_index("row"), 2)


def join_kernel(first, second, pair):
    inner = first.shape[0]
    pair[:inner, :] = first[...]
    pair[inner:, :] = second[...]


def split(value):
    high = value.astype(BF16)
    low = (value - high.astype(F32)).astype(BF16)
    return high, low


dot = functools.partial(jnp.dot, preferred_element_type=F32)


def product(left_high, left_low, right_high, right_low):
    return dot(left_high, right_high) + (dot(left_high, right_low) + dot(left_low, right_high))


def take_left(index, block, left_high, left_low):
    rows = pl.ds(index * TILE, TILE)
    high, low = split(block[...].T)
    left_high[rows, :] = high
    left_low[rows, :] = low


def take_right(index, parity, block, right_high, right_low):
    start = 2 * index * TILE + parity * TILE
    columns = pl.ds(start if isinstance(start, int) else pl.multiple_of(start, TILE), TILE)
    high, low = split(block[...])
    right_high[:, columns] = high
    right_low[:, columns] = low


def place(index, first, second, first_swapped, second_swapped, left, right):
    @pl.when(core() == 0)
    def _():
        take_left(index, first, *left)
        take_right(index, 0, second_swapped, *right)
        take_right(index, 1, first_swapped, *right)

    @pl.when(core() == 1)
    def _():
        take_left(index, second_swapped, *left)
        take_right(index, 0, second, *right)
        take_right(index, 1, first, *right)


def halves(pair):
    inner = pair.shape[0] // 2
    return pair.at[pl.ds(0, inner), :], pair.at[pl.ds(inner, inner), :]


def first_product_kernel(own, other, o1, s1, o3, s3, oo, ss, left_high, left_low, right_high, right_low, total):
    left, right = (left_high, left_low), (right_high, right_low)
    take_left(0, own, *left)
    take_right(0, core(), own, *right)
    take_right(0, 1 - core(), other, *right)
    (o1_swapped, o3_swapped), (s1_swapped, s3_swapped) = halves(oo), halves(ss)
    place(1, o1, s1, o1_swapped, s1_swapped, left, right)
    place(2, o3, s3, o3_swapped, s3_swapped, left, right)
    for index in range(3):
        columns = pl.ds(index * 2 * TILE, 2 * TILE)
        total[:, columns] = product(left_high[...], left_low[...], right_high[:, columns], right_low[:, columns])


def turn():
    return 1 - 2 * core()


def strip(index):
    return pl.ds(pl.multiple_of(index * SUB, SUB), SUB)


def scatter(total, outs):
    z = lax.axis_index("layer")
    for shift, out in zip((0, 1, 3, 2), outs):
        s = lax.rem(z + shift, 4)
        for index in range(4):
            out[pl.ds(index * SUB, SUB), :] = total[strip(index * 4 + s), :]


def second_product_kernel(o2, s2, both, right_high, right_low, part, *refs):
    outs, (last_high, last_low, total) = refs[:4], refs[4:]
    swapped = both.at[pl.ds(s2.shape[0], s2.shape[0]), :]

    @pl.when(core() == 0)
    def _():
        take_left(0, o2, last_high, last_low)

    @pl.when(core() == 1)
    def _():
        take_left(0, swapped, last_high, last_low)

    known, columns = part.shape[0], pl.ds(0, total.shape[1])
    total[:known, :] = part[:, columns]
    total[known:, :] = product(last_high[...], last_low[...], right_high[:, columns], right_low[:, columns])
    scatter(total, outs)


def third_product_kernel(o2, s2, both, last_high, last_low, left_high, left_low, right_high, right_low, part, *refs):
    outs, (far_high, far_low, total) = refs[:4], refs[4:]
    o2_swapped, s2_swapped = halves(both)

    @pl.when(core() == 0)
    def _():
        take_right(0, 0, s2_swapped, far_high, far_low)
        take_right(0, 1, o2_swapped, far_high, far_low)

    @pl.when(core() == 1)
    def _():
        take_right(0, 0, s2, far_high, far_low)
        take_right(0, 1, o2, far_high, far_low)

    known, wide = part.shape[0], 2 * TILE
    columns = pl.ds(part.shape[1] - wide, wide)
    total[:known, :wide] = part[:, columns]
    total[known:, :wide] = product(last_high[...], last_low[...], right_high[:, columns], right_low[:, columns])
    total[:known, wide:] = product(left_high[...], left_low[...], far_high[...], far_low[...])
    total[known:, wide:] = product(last_high[...], last_low[...], far_high[...], far_low[...])
    scatter(total, outs)


def group_kernel(mine, below, above, two, own, up, far, down):
    group, y = lax.axis_index("layer") // 4, lax.axis_index("col")
    for i, out in enumerate((own, up, far, down)):
        t = lax.rem(group + i - y + 4, 4)
        rows = strip(jnp.where(t < 2, t, 5 - t))
        out[...] = (mine[rows, :] + two[rows, :]) + (below[rows, :] + above[rows, :])


def up_kernel(first, second, came, out):
    half = first.shape[1]
    out[:, :half] = first[...] + came[...]
    out[:, half:] = second[...]


def add_kernel(held, came, out):
    out[...] = held[...] + came[...]


def below_kernel(first, second, from_below, out):
    half = first.shape[1]
    out[:, :half] = first[...] + from_below[:, :half]
    out[:, half:] = second[...] + from_below[:, half:]


def last_kernel(held, above, out):
    x, half = lax.axis_index("row") // 2, held.shape[1] // 2
    for index, t in enumerate(ORDER):
        source = pl.ds(index * 2 * TILE, 2 * TILE)
        target = pl.ds(pl.multiple_of(lax.rem(x + t, N_X) * 2 * TILE, 2 * TILE), 2 * TILE)
        value = held[:, source]
        if index >= 2:
            value = value + above[:, pl.ds(index * 2 * TILE - half, 2 * TILE)]
        out[:, target] = value


def swap(value):
    return lax.ppermute(value, "row", [(i, i ^ 1) for i in range(N_ROW)])


def fetch(value, t):
    pairs = []
    for x in range(N_X):
        for y in range(N_COL):
            pairs.append(((2 * x) * N_COL + (y + t) % N_COL, (2 * x) * N_COL + y))
            pairs.append(((2 * ((x + t) % N_X) + 1) * N_COL + y, (2 * x + 1) * N_COL + y))
    return lax.ppermute(value, ("row", "col"), pairs)


def pass_on(value, distance):
    pairs = []
    for z in range(N_LAYER):
        for row in range(N_ROW):
            to = (z + (distance if row % 2 == 0 else -distance)) % N_LAYER
            pairs.append((z * N_ROW + row, to * N_ROW + row))
    return lax.ppermute(value, ("layer", "row"), pairs)


def shift_layers(value, distance):
    return lax.ppermute(value, "layer", [(z, (z + distance) % N_LAYER) for z in range(N_LAYER)])


def on_device(graph, pattern):
    inner = graph.shape[0]
    (masked,) = call(mask_kernel, [(inner, TILE)], (graph, pattern.reshape(-1)), [VMEM, SMEM])
    other = swap(masked)
    o1, o3 = fetch(masked, 1), fetch(masked, 3)
    s3, s1 = fetch(other, 3), fetch(other, 1)
    o2, s2 = fetch(o1, 1), fetch(s3, 3)

    def swap_two(first, second):
        return swap(call(join_kernel, [(2 * inner, TILE)], (first, second))[0])

    known, wide = 3 * TILE, 6 * TILE
    parts = call(
        first_product_kernel,
        [((known, inner), BF16)] * 2 + [((inner, wide), BF16)] * 2 + [(known, wide)],
        (masked, other, o1, s1, o3, s3, swap_two(o1, o3), swap_two(s1, s3)),
        flops=6 * known * wide * inner,
        nbytes=8 << 20,
    )
    left_high, left_low, right_high, right_low, part = parts
    second = (o2, s2, swap_two(o2, s2))
    outs = [(4 * SUB, 4 * TILE)] * 4
    total = pltpu.VMEM((4 * TILE, 4 * TILE), F32)
    *cut_a, last_high, last_low = call(
        second_product_kernel,
        outs + [((TILE, inner), BF16)] * 2,
        (*second, right_high, right_low, part),
        scratch=[total],
        flops=6 * TILE * 4 * TILE * inner,
        nbytes=4 << 20,
    )
    cut_b = call(
        third_product_kernel,
        outs,
        (*second, last_high, last_low, left_high, left_low, right_high, right_low, part),
        scratch=[pltpu.VMEM((inner, 2 * TILE), BF16)] * 2 + [total],
        flops=6 * 5 * TILE * 2 * TILE * inner,
        nbytes=4 << 20,
    )

    def neighbours(cut):
        return cut[0], shift_layers(cut[1], 1), shift_layers(cut[2], -1), pass_on(cut[3], 2)

    piece, chunk = (SUB, 4 * TILE), (SUB, 8 * TILE)
    own_a, up_a, far_a, down_a = call(group_kernel, [piece] * 4, neighbours(cut_a))
    own_b, up_b, far_b, down_b = call(group_kernel, [piece] * 4, neighbours(cut_b), after=own_a)
    (up,) = call(up_kernel, [chunk], (up_a, up_b, shift_layers(far_a, 4)), flops=1 << 30)
    (own_a,) = call(add_kernel, [piece], (own_a, shift_layers(down_a, -4)))
    (down,) = call(add_kernel, [piece], (down_b, shift_layers(far_b, -4)), flops=1 << 30, after=own_a)
    (held,) = call(below_kernel, [chunk], (own_a, own_b, shift_layers(up, 4)))
    return call(last_kernel, [chunk], (held, shift_layers(down, -4)))[0]


def solution(mesh):
    placed = (P("layer", ("row", "col")), P("layer", ("row", "col")))
    return jax.shard_map(
        on_device, mesh=mesh, in_specs=placed, out_specs=P(("row", "layer"), "col"), check_vma=False
    )
```

```python
import functools

import jax
import jax.numpy as jnp
from jax import lax
from jax.experimental import pallas as pl
from jax.experimental.pallas import tpu as pltpu
from jax.sharding import PartitionSpec as P

TILE = 128
N_LAYER = 16
N_X = 4
N_ROW = 8
N_COL = 4
SUB = 32
ORDER = (0, 1, 3, 2)
VMEM = pl.BlockSpec(memory_space=pltpu.VMEM)
SMEM = pl.BlockSpec(memory_space=pltpu.SMEM)
LIMIT = 40 * 1024 * 1024
F32, BF16 = jnp.float32, jnp.bfloat16


def call(kernel, outs, operands, specs=None, scratch=(), flops=0, nbytes=1 << 20, after=None, limit=LIMIT):
    if after is not None:
        inner_kernel, count = kernel, len(operands)
        kernel = lambda *refs: inner_kernel(*refs[:count], *refs[count + 1 :])
        specs = [VMEM] * count + [pl.BlockSpec(memory_space=pl.ANY)]
        operands = (*operands, after)
    outs = [o if isinstance(o[0], tuple) else (o, F32) for o in outs]
    return pl.pallas_call(
        kernel,
        out_shape=tuple(jax.ShapeDtypeStruct(s, d) for s, d in outs),
        in_specs=specs or [VMEM] * len(operands),
        out_specs=tuple(VMEM for _ in outs),
        scratch_shapes=list(scratch),
        compiler_params=pltpu.CompilerParams(vmem_limit_bytes=limit),
        cost_estimate=pl.CostEstimate(flops=flops, bytes_accessed=nbytes, transcendentals=0),
    )(*operands)


def mask_kernel(graph, pattern, masked, raw, flags, sems):
    tiles = graph.shape[0] // TILE
    flag_copy = pltpu.make_async_copy(pattern, flags, sems.at[tiles])
    flag_copy.start()
    copies = []
    for k in range(tiles):
        rows = pl.ds(k * TILE, TILE)
        copies.append(pltpu.make_async_copy(graph.at[rows, :], raw.at[rows, :], sems.at[k]))
        copies[k].start()
    flag_copy.wait()
    for k in range(tiles):
        rows = pl.ds(k * TILE, TILE)
        copies[k].wait()
        masked[rows, :] = raw[rows, :] * flags[k].astype(F32)


def core():
    return lax.rem(lax.axis_index("row"), 2)


def join_kernel(first, second, pair):
    inner = first.shape[0]
    pair[:inner, :] = first[...]
    pair[inner:, :] = second[...]


def split(value):
    high = value.astype(BF16)
    low = (value - high.astype(F32)).astype(BF16)
    return high, low


dot = functools.partial(jnp.dot, preferred_element_type=F32)


def product(left_high, left_low, right_high, right_low):
    return dot(left_high, right_high) + (dot(left_high, right_low) + dot(left_low, right_high))


def take_left(index, block, left_high, left_low):
    rows = pl.ds(index * TILE, TILE)
    high, low = split(block[...].T)
    left_high[rows, :] = high
    left_low[rows, :] = low


def take_right(index, parity, block, right_high, right_low):
    start = 2 * index * TILE + parity * TILE
    columns = pl.ds(start if isinstance(start, int) else pl.multiple_of(start, TILE), TILE)
    high, low = split(block[...])
    right_high[:, columns] = high
    right_low[:, columns] = low


def place(index, first, second, first_swapped, second_swapped, left, right):
    @pl.when(core() == 0)
    def _():
        take_left(index, first, *left)
        take_right(index, 0, second_swapped, *right)
        take_right(index, 1, first_swapped, *right)

    @pl.when(core() == 1)
    def _():
        take_left(index, second_swapped, *left)
        take_right(index, 0, second, *right)
        take_right(index, 1, first, *right)


def halves(pair):
    inner = pair.shape[0] // 2
    return pair.at[pl.ds(0, inner), :], pair.at[pl.ds(inner, inner), :]


def first_product_kernel(own, other, o1, s1, o3, s3, o1_s3, o3_s1, left_high, left_low, right_high, right_low, total):
    left, right = (left_high, left_low), (right_high, right_low)
    take_left(0, own, *left)
    take_right(0, core(), own, *right)
    take_right(0, 1 - core(), other, *right)
    (o1_swapped, s3_swapped), (o3_swapped, s1_swapped) = halves(o1_s3), halves(o3_s1)
    place(1, o1, s1, o1_swapped, s1_swapped, left, right)
    place(2, o3, s3, o3_swapped, s3_swapped, left, right)
    for index in range(3):
        columns = pl.ds(index * 2 * TILE, 2 * TILE)
        total[:, columns] = product(left_high[...], left_low[...], right_high[:, columns], right_low[:, columns])


def turn():
    return 1 - 2 * core()


def strip(index):
    return pl.ds(pl.multiple_of(index * SUB, SUB), SUB)


def scatter(total, send, keep):
    z, y = lax.axis_index("layer"), lax.axis_index("col")

    def rows_of(layer):
        t = lax.rem(layer // 4 - y + N_COL, N_COL)
        index = jnp.where(t < 2, t, 5 - t)
        return strip(index * 4 + lax.rem(layer, 4))

    for j in range(N_LAYER // 2):
        rows = pl.ds(j * SUB, SUB)
        keep[rows, :] = total[rows_of(lax.rem(z + 2 * j, N_LAYER)), :]
        send[rows, :] = total[rows_of(lax.rem(z + turn() + 2 * j + N_LAYER, N_LAYER)), :]


def second_product_kernel(o2, s2, both, right_high, right_low, part, send, keep, last_high, last_low, total):
    swapped = both.at[pl.ds(s2.shape[0], s2.shape[0]), :]

    @pl.when(core() == 0)
    def _():
        take_left(0, o2, last_high, last_low)

    @pl.when(core() == 1)
    def _():
        take_left(0, swapped, last_high, last_low)

    known, columns = part.shape[0], pl.ds(0, total.shape[1])
    total[:known, :] = part[:, columns]
    total[known:, :] = product(last_high[...], last_low[...], right_high[:, columns], right_low[:, columns])
    scatter(total, send, keep)


def third_product_kernel(o2, s2, both, last_high, last_low, left_high, left_low, right_high, right_low, part, *refs):
    send, keep, far_high, far_low, total = refs
    o2_swapped, s2_swapped = halves(both)

    @pl.when(core() == 0)
    def _():
        take_right(0, 0, s2_swapped, far_high, far_low)
        take_right(0, 1, o2_swapped, far_high, far_low)

    @pl.when(core() == 1)
    def _():
        take_right(0, 0, s2, far_high, far_low)
        take_right(0, 1, o2, far_high, far_low)

    known, wide = part.shape[0], 2 * TILE
    columns = pl.ds(part.shape[1] - wide, wide)
    total[:known, :wide] = part[:, columns]
    total[known:, :wide] = product(last_high[...], last_low[...], right_high[:, columns], right_low[:, columns])
    total[:known, wide:] = product(left_high[...], left_low[...], far_high[...], far_low[...])
    total[known:, wide:] = product(last_high[...], last_low[...], far_high[...], far_low[...])
    scatter(total, send, keep)


def stage_kernel(held, came, send, keep):
    count = held.shape[0] // SUB
    for i in range(count // 2):
        rows = pl.ds(i * SUB, SUB)
        near = pl.ds(2 * i * SUB, SUB)
        far = strip(lax.rem(turn() + 2 * i + count, count))
        keep[rows, :] = held[near, :] + came[near, :]
        send[rows, :] = held[far, :] + came[far, :]


def group_kernel(held, came, own, up, far, down):
    for i, out in enumerate((own, up, far, down)):
        rows = pl.ds(i * SUB, SUB)
        out[...] = held[rows, :] + came[rows, :]


def up_kernel(first, second, came, out):
    half = first.shape[1]
    out[:, :half] = first[...] + came[...]
    out[:, half:] = second[...]


def down_kernel(first, second, came, out):
    half = first.shape[1]
    out[:, :half] = first[...]
    out[:, half:] = second[...] + came[...]


def below_kernel(first, second, from_below, out):
    half = first.shape[1]
    out[:, :half] = first[...] + from_below[:, :half]
    out[:, half:] = second[...] + from_below[:, half:]


def last_kernel(held, from_above, out):
    x = lax.axis_index("row") // 2
    for index, t in enumerate(ORDER):
        source = pl.ds(index * 2 * TILE, 2 * TILE)
        target = pl.ds(pl.multiple_of(lax.rem(x + t, N_X) * 2 * TILE, 2 * TILE), 2 * TILE)
        out[:, target] = held[:, source] + from_above[:, source]


def swap(value):
    return lax.ppermute(value, "row", [(i, i ^ 1) for i in range(N_ROW)])


def fetch(value, t):
    pairs = []
    for x in range(N_X):
        for y in range(N_COL):
            pairs.append(((2 * x) * N_COL + (y + t) % N_COL, (2 * x) * N_COL + y))
            pairs.append(((2 * ((x + t) % N_X) + 1) * N_COL + y, (2 * x + 1) * N_COL + y))
    return lax.ppermute(value, ("row", "col"), pairs)


def pass_on(value, distance):
    pairs = []
    for z in range(N_LAYER):
        for row in range(N_ROW):
            to = (z + (distance if row % 2 == 0 else -distance)) % N_LAYER
            pairs.append((z * N_ROW + row, to * N_ROW + row))
    return lax.ppermute(value, ("layer", "row"), pairs)


def shift_layers(value, distance):
    return lax.ppermute(value, "layer", [(z, (z + distance) % N_LAYER) for z in range(N_LAYER)])


def on_device(graph, pattern):
    inner = graph.shape[0]
    tiles = inner // TILE
    (masked,) = call(
        mask_kernel,
        [(inner, TILE)],
        (graph, pattern.reshape(-1)),
        [pl.BlockSpec(memory_space=pltpu.HBM)] * 2,
        scratch=[
            pltpu.VMEM((inner, TILE), F32),
            pltpu.SMEM((tiles,), jnp.int32),
            pltpu.SemaphoreType.DMA((tiles + 1,)),
        ],
        limit=62 * 1024 * 1024,
    )
    other = swap(masked)
    o1, o3 = fetch(masked, 1), fetch(masked, 3)
    s3, s1 = fetch(other, 3), fetch(other, 1)
    o2, s2 = fetch(o1, 1), fetch(s3, 3)

    def swap_two(first, second, after=None):
        return swap(call(join_kernel, [(2 * inner, TILE)], (first, second), after=after)[0])

    known, wide = 3 * TILE, 6 * TILE
    parts = call(
        first_product_kernel,
        [((known, inner), BF16)] * 2 + [((inner, wide), BF16)] * 2 + [(known, wide)],
        (masked, other, o1, s1, o3, s3, swap_two(o1, s3), swap_two(o3, s1)),
        nbytes=1 << 10,
    )
    left_high, left_low, right_high, right_low, part = parts
    second = (o2, s2, swap_two(o2, s2))
    out = (8 * SUB, 4 * TILE)
    total = pltpu.VMEM((4 * TILE, 4 * TILE), F32)
    send_a, keep_a, *last = call(
        second_product_kernel,
        [out, out, ((TILE, inner), BF16), ((TILE, inner), BF16)],
        (*second, right_high, right_low, part),
        scratch=[total],
        flops=6 * TILE * 4 * TILE * inner,
        nbytes=4 << 20,
    )
    send_b, keep_b = call(
        third_product_kernel,
        [out, out],
        (*second, *last, left_high, left_low, right_high, right_low, part),
        scratch=[pltpu.VMEM((inner, 2 * TILE), BF16)] * 2 + [total],
        flops=6 * 5 * TILE * 2 * TILE * inner,
        nbytes=4 << 20,
    )
    sends, keeps = [send_a, send_b], [keep_a, keep_b]
    arrived = [pass_on(sends[half], 1) for half in range(2)]
    done = None
    for half in range(2):
        sends[half], keeps[half] = call(
            stage_kernel, [(4 * SUB, 4 * TILE)] * 2, (keeps[half], arrived[half]), after=done
        )
        done = keeps[half]
        arrived[half] = pass_on(sends[half], 2)
    first = call(group_kernel, [(SUB, 4 * TILE)] * 4, (keeps[0], arrived[0]))
    second = call(group_kernel, [(SUB, 4 * TILE)] * 4, (keeps[1], arrived[1]), after=first[0])
    chunk = [(SUB, 8 * TILE)]
    (up,) = call(up_kernel, chunk, (first[1], second[1], shift_layers(first[2], 4)))
    (down,) = call(down_kernel, chunk, (first[3], second[3], shift_layers(second[2], -4)), after=up)
    (held,) = call(below_kernel, chunk, (first[0], second[0], shift_layers(up, 4)))
    return call(last_kernel, chunk, (held, shift_layers(down, -4)))[0]


def solution(mesh):
    placed = (P("layer", ("row", "col")), P("layer", ("row", "col")))
    return jax.shard_map(
        on_device, mesh=mesh, in_specs=placed, out_specs=P(("row", "layer"), "col"), check_vma=False
    )
```

```python
import functools

import jax
import jax.numpy as jnp
from jax import lax
from jax.experimental import pallas as pl
from jax.experimental.pallas import tpu as pltpu
from jax.sharding import PartitionSpec as P

TILE = 128
N_LAYER = 16
N_X = 4
N_ROW = 8
N_COL = 4
SUB = 32
ORDER = (0, 1, 3, 2)
VMEM = pl.BlockSpec(memory_space=pltpu.VMEM)
SMEM = pl.BlockSpec(memory_space=pltpu.SMEM)
LIMIT = 40 * 1024 * 1024
F32, BF16 = jnp.float32, jnp.bfloat16


def call(kernel, outs, operands, specs=None, scratch=(), flops=0, nbytes=1 << 20, after=None, limit=LIMIT):
    if after is not None:
        inner_kernel, count = kernel, len(operands)
        kernel = lambda *refs: inner_kernel(*refs[:count], *refs[count + 1 :])
        specs = [VMEM] * count + [pl.BlockSpec(memory_space=pl.ANY)]
        operands = (*operands, after)
    outs = [o if isinstance(o[0], tuple) else (o, F32) for o in outs]
    return pl.pallas_call(
        kernel,
        out_shape=tuple(jax.ShapeDtypeStruct(s, d) for s, d in outs),
        in_specs=specs or [VMEM] * len(operands),
        out_specs=tuple(VMEM for _ in outs),
        scratch_shapes=list(scratch),
        compiler_params=pltpu.CompilerParams(vmem_limit_bytes=limit),
        cost_estimate=pl.CostEstimate(flops=flops, bytes_accessed=nbytes, transcendentals=0),
    )(*operands)


def mask_kernel(graph, pattern, masked, raw, flags, sems):
    tiles = graph.shape[0] // TILE
    flag_copy = pltpu.make_async_copy(pattern, flags, sems.at[tiles])
    flag_copy.start()
    copies = []
    for k in range(tiles):
        rows = pl.ds(k * TILE, TILE)
        copies.append(pltpu.make_async_copy(graph.at[rows, :], raw.at[rows, :], sems.at[k]))
        copies[k].start()
    flag_copy.wait()
    for k in range(tiles):
        rows = pl.ds(k * TILE, TILE)
        copies[k].wait()
        masked[rows, :] = raw[rows, :] * flags[k].astype(F32)


def core():
    return lax.rem(lax.axis_index("row"), 2)


def join_kernel(first, second, pair):
    inner = first.shape[0]
    pair[:inner, :] = first[...]
    pair[inner:, :] = second[...]


def split(value):
    high = value.astype(BF16)
    low = (value - high.astype(F32)).astype(BF16)
    return high, low


dot = functools.partial(jnp.dot, preferred_element_type=F32)


def product(left_high, left_low, right_high, right_low):
    return dot(left_high, right_high) + (dot(left_high, right_low) + dot(left_low, right_high))


def take_left(index, block, left_high, left_low):
    rows = pl.ds(index * TILE, TILE)
    high, low = split(block[...].T)
    left_high[rows, :] = high
    left_low[rows, :] = low


def take_right(index, parity, block, right_high, right_low):
    start = 2 * index * TILE + parity * TILE
    columns = pl.ds(start if isinstance(start, int) else pl.multiple_of(start, TILE), TILE)
    high, low = split(block[...])
    right_high[:, columns] = high
    right_low[:, columns] = low


def halves(pair):
    inner = pair.shape[0] // 2
    return pair.at[pl.ds(0, inner), :], pair.at[pl.ds(inner, inner), :]


def early_product_kernel(own, other, o1, s1, o3, s3, left_high, left_low, right_high, right_low, total):
    left, right = (left_high, left_low), (right_high, right_low)
    take_left(0, own, *left)
    take_right(0, core(), own, *right)
    take_right(0, 1 - core(), other, *right)

    @pl.when(core() == 0)
    def _():
        take_left(1, o1, *left)
        take_left(2, o3, *left)
        columns = pl.ds(0, 2 * TILE)
        total[:, columns] = product(left_high[...], left_low[...], right_high[:, columns], right_low[:, columns])

    @pl.when(core() == 1)
    def _():
        for index, o, s in ((1, o1, s1), (2, o3, s3)):
            take_right(index, 0, s, *right)
            take_right(index, 1, o, *right)
        rows = pl.ds(0, TILE)
        total[rows, :] = product(left_high[rows, :], left_low[rows, :], right_high[...], right_low[...])


def first_product_kernel(o1_s3, o3_s1, early_left, early_left_low, early_right, early_right_low, *refs):
    left_high, left_low, right_high, right_low, beside, below = refs
    (o1, s3), (o3, s1) = halves(o1_s3), halves(o3_s1)

    @pl.when(core() == 0)
    def _():
        for index, o, s in ((0, o1, s1), (1, o3, s3)):
            take_right(index, 0, s, right_high, right_low)
            take_right(index, 1, o, right_high, right_low)
        beside[...] = product(early_left[...], early_left_low[...], right_high[...], right_low[...])

    @pl.when(core() == 1)
    def _():
        take_left(0, s1, left_high, left_low)
        take_left(1, s3, left_high, left_low)
        below[...] = product(left_high[...], left_low[...], early_right[...], early_right_low[...])


def turn():
    return 1 - 2 * core()


def strip(index):
    return pl.ds(pl.multiple_of(index * SUB, SUB), SUB)


def scatter(total, send, keep):
    z, y = lax.axis_index("layer"), lax.axis_index("col")

    def rows_of(layer):
        t = lax.rem(layer // 4 - y + N_COL, N_COL)
        index = jnp.where(t < 2, t, 5 - t)
        return strip(index * 4 + lax.rem(layer, 4))

    for j in range(N_LAYER // 2):
        rows = pl.ds(j * SUB, SUB)
        keep[rows, :] = total[rows_of(lax.rem(z + 2 * j, N_LAYER)), :]
        send[rows, :] = total[rows_of(lax.rem(z + turn() + 2 * j + N_LAYER, N_LAYER)), :]


def second_product_kernel(o2, s2, both, early_right, early_right_low, early, right_high, right_low, beside, below, *refs):
    send, keep, last_high, last_low, total = refs
    known, wide = early.shape[0], 2 * TILE
    first, next_ = pl.ds(0, wide), pl.ds(wide, wide)

    def last_rows(columns, high, low):
        total[known:, columns] = product(last_high[...], last_low[...], high, low)

    @pl.when(core() == 0)
    def _():
        take_left(0, o2, last_high, last_low)
        total[:known, first] = early[:, first]
        total[:known, next_] = beside[:, first]
        last_rows(first, early_right[:, first], early_right_low[:, first])
        last_rows(next_, right_high[:, first], right_low[:, first])

    @pl.when(core() == 1)
    def _():
        columns = pl.ds(0, 2 * wide)
        take_left(0, both.at[pl.ds(s2.shape[0], s2.shape[0]), :], last_high, last_low)
        total[:TILE, :] = early[:TILE, columns]
        total[TILE:known, :] = below[:, columns]
        last_rows(columns, early_right[:, columns], early_right_low[:, columns])

    scatter(total, send, keep)


def third_product_kernel(o2, s2, both, last_high, last_low, *refs):
    early_left, early_left_low, early_right, early_right_low, early = refs[:5]
    left_high, left_low, right_high, right_low, beside, below = refs[5:11]
    send, keep, far_high, far_low, total = refs[11:]
    o2_swapped, s2_swapped = halves(both)
    known, wide = early.shape[0], 2 * TILE
    first, next_, third = (pl.ds(i * wide, wide) for i in range(3))

    def far(rows, high, low):
        total[rows, next_] = product(high, low, far_high[...], far_low[...])

    @pl.when(core() == 0)
    def _():
        take_right(0, 0, s2_swapped, far_high, far_low)
        take_right(0, 1, o2_swapped, far_high, far_low)
        total[:known, first] = beside[:, next_]
        total[known:, first] = product(last_high[...], last_low[...], right_high[:, next_], right_low[:, next_])
        far(pl.ds(0, known), early_left[...], early_left_low[...])
        far(pl.ds(known, TILE), last_high[...], last_low[...])

    @pl.when(core() == 1)
    def _():
        take_right(0, 0, s2, far_high, far_low)
        take_right(0, 1, o2, far_high, far_low)
        total[:TILE, first] = early[:TILE, third]
        total[TILE:known, first] = below[:, third]
        total[known:, first] = product(last_high[...], last_low[...], early_right[:, third], early_right_low[:, third])
        far(pl.ds(0, TILE), early_left[:TILE, :], early_left_low[:TILE, :])
        far(pl.ds(TILE, known - TILE), left_high[...], left_low[...])
        far(pl.ds(known, TILE), last_high[...], last_low[...])

    scatter(total, send, keep)


def stage_kernel(held, came, send, keep):
    count = held.shape[0] // SUB
    for i in range(count // 2):
        rows = pl.ds(i * SUB, SUB)
        near = pl.ds(2 * i * SUB, SUB)
        far = strip(lax.rem(turn() + 2 * i + count, count))
        keep[rows, :] = held[near, :] + came[near, :]
        send[rows, :] = held[far, :] + came[far, :]


def group_kernel(held, came, own, up, far, down):
    for i, out in enumerate((own, up, far, down)):
        rows = pl.ds(i * SUB, SUB)
        out[...] = held[rows, :] + came[rows, :]


def up_kernel(first, second, came, out):
    half = first.shape[1]
    out[:, :half] = first[...] + came[...]
    out[:, half:] = second[...]


def down_kernel(first, second, came, out):
    half = first.shape[1]
    out[:, :half] = first[...]
    out[:, half:] = second[...] + came[...]


def below_kernel(first, second, from_below, out):
    half = first.shape[1]
    out[:, :half] = first[...] + from_below[:, :half]
    out[:, half:] = second[...] + from_below[:, half:]


def last_kernel(held, from_above, out):
    x = lax.axis_index("row") // 2
    for index, t in enumerate(ORDER):
        source = pl.ds(index * 2 * TILE, 2 * TILE)
        target = pl.ds(pl.multiple_of(lax.rem(x + t, N_X) * 2 * TILE, 2 * TILE), 2 * TILE)
        out[:, target] = held[:, source] + from_above[:, source]


def swap(value):
    return lax.ppermute(value, "row", [(i, i ^ 1) for i in range(N_ROW)])


def fetch(value, t):
    pairs = []
    for x in range(N_X):
        for y in range(N_COL):
            pairs.append(((2 * x) * N_COL + (y + t) % N_COL, (2 * x) * N_COL + y))
            pairs.append(((2 * ((x + t) % N_X) + 1) * N_COL + y, (2 * x + 1) * N_COL + y))
    return lax.ppermute(value, ("row", "col"), pairs)


def pass_on(value, distance):
    pairs = []
    for z in range(N_LAYER):
        for row in range(N_ROW):
            to = (z + (distance if row % 2 == 0 else -distance)) % N_LAYER
            pairs.append((z * N_ROW + row, to * N_ROW + row))
    return lax.ppermute(value, ("layer", "row"), pairs)


def shift_layers(value, distance):
    return lax.ppermute(value, "layer", [(z, (z + distance) % N_LAYER) for z in range(N_LAYER)])


def on_device(graph, pattern):
    inner = graph.shape[0]
    tiles = inner // TILE
    (masked,) = call(
        mask_kernel,
        [(inner, TILE)],
        (graph, pattern.reshape(-1)),
        [pl.BlockSpec(memory_space=pltpu.HBM)] * 2,
        scratch=[
            pltpu.VMEM((inner, TILE), F32),
            pltpu.SMEM((tiles,), jnp.int32),
            pltpu.SemaphoreType.DMA((tiles + 1,)),
        ],
        limit=62 * 1024 * 1024,
    )
    other = swap(masked)
    o1, o3 = fetch(masked, 1), fetch(masked, 3)
    s3, s1 = fetch(other, 3), fetch(other, 1)
    o2, s2 = fetch(o1, 1), fetch(s3, 3)

    def swap_two(first, second, after=None):
        return swap(call(join_kernel, [(2 * inner, TILE)], (first, second), after=after)[0])

    known, wide = 3 * TILE, 6 * TILE
    shapes = [((known, inner), BF16)] * 2 + [((inner, wide), BF16)] * 2 + [(known, wide)]
    early = call(early_product_kernel, shapes, (masked, other, o1, s1, o3, s3), nbytes=1 << 10)
    second = (o2, s2, swap_two(o2, s2, after=early[4]))
    late = call(
        first_product_kernel,
        [((known - TILE, inner), BF16)] * 2
        + [((inner, wide - 2 * TILE), BF16)] * 2
        + [(known, wide - 2 * TILE), (known - TILE, wide)],
        (swap_two(o1, s3), swap_two(o3, s1), *early[:4]),
        flops=4 * known * wide * inner,
        nbytes=8 << 20,
    )
    out = (8 * SUB, 4 * TILE)
    total = pltpu.VMEM((4 * TILE, 4 * TILE), F32)
    send_a, keep_a, *last = call(
        second_product_kernel,
        [out, out, ((TILE, inner), BF16), ((TILE, inner), BF16)],
        (*second, *early[2:], *late[2:]),
        scratch=[total],
        flops=6 * TILE * 4 * TILE * inner,
        nbytes=4 << 20,
    )
    send_b, keep_b = call(
        third_product_kernel,
        [out, out],
        (*second, *last, *early, *late),
        scratch=[pltpu.VMEM((inner, 2 * TILE), BF16)] * 2 + [total],
        flops=6 * 5 * TILE * 2 * TILE * inner,
        nbytes=4 << 20,
    )
    sends, keeps = [send_a, send_b], [keep_a, keep_b]
    arrived = [pass_on(sends[half], 1) for half in range(2)]
    done = None
    for half in range(2):
        sends[half], keeps[half] = call(
            stage_kernel, [(4 * SUB, 4 * TILE)] * 2, (keeps[half], arrived[half]), after=done
        )
        done = keeps[half]
        arrived[half] = pass_on(sends[half], 2)
    first = call(group_kernel, [(SUB, 4 * TILE)] * 4, (keeps[0], arrived[0]))
    second = call(group_kernel, [(SUB, 4 * TILE)] * 4, (keeps[1], arrived[1]), after=first[0])
    chunk = [(SUB, 8 * TILE)]
    (up,) = call(up_kernel, chunk, (first[1], second[1], shift_layers(first[2], 4)))
    (down,) = call(down_kernel, chunk, (first[3], second[3], shift_layers(second[2], -4)), after=up)
    (held,) = call(below_kernel, chunk, (first[0], second[0], shift_layers(up, 4)))
    return call(last_kernel, chunk, (held, shift_layers(down, -4)))[0]


def solution(mesh):
    placed = (P("layer", ("row", "col")), P("layer", ("row", "col")))
    return jax.shard_map(
        on_device, mesh=mesh, in_specs=placed, out_specs=P(("row", "layer"), "col"), check_vma=False
    )
```

```python
import functools

import jax
import jax.numpy as jnp
from jax import lax
from jax.experimental import pallas as pl
from jax.experimental.pallas import tpu as pltpu
from jax.sharding import PartitionSpec as P

TILE = 128
N_LAYER = 16
N_X = 4
N_ROW = 8
N_COL = 4
SUB = 32
ORDER = (0, 1, 3, 2)
VMEM = pl.BlockSpec(memory_space=pltpu.VMEM)
SMEM = pl.BlockSpec(memory_space=pltpu.SMEM)
LIMIT = 40 * 1024 * 1024
F32, BF16 = jnp.float32, jnp.bfloat16


def call(kernel, outs, operands, specs=None, scratch=(), flops=0, nbytes=1 << 20, after=None, limit=LIMIT):
    if after is not None:
        inner_kernel, count = kernel, len(operands)
        kernel = lambda *refs: inner_kernel(*refs[:count], *refs[count + 1 :])
        specs = [VMEM] * count + [pl.BlockSpec(memory_space=pl.ANY)]
        operands = (*operands, after)
    outs = [o if isinstance(o[0], tuple) else (o, F32) for o in outs]
    return pl.pallas_call(
        kernel,
        out_shape=tuple(jax.ShapeDtypeStruct(s, d) for s, d in outs),
        in_specs=specs or [VMEM] * len(operands),
        out_specs=tuple(VMEM for _ in outs),
        scratch_shapes=list(scratch),
        compiler_params=pltpu.CompilerParams(vmem_limit_bytes=limit),
        cost_estimate=pl.CostEstimate(flops=flops, bytes_accessed=nbytes, transcendentals=0),
    )(*operands)


def mask_kernel(graph, pattern, masked, raw, flags, sems):
    tiles = graph.shape[0] // TILE
    flag_copy = pltpu.make_async_copy(pattern, flags, sems.at[tiles])
    flag_copy.start()
    copies = []
    for k in range(tiles):
        rows = pl.ds(k * TILE, TILE)
        copies.append(pltpu.make_async_copy(graph.at[rows, :], raw.at[rows, :], sems.at[k]))
        copies[k].start()
    flag_copy.wait()
    for k in range(tiles):
        rows = pl.ds(k * TILE, TILE)
        copies[k].wait()
        masked[rows, :] = raw[rows, :] * flags[k].astype(F32)


def core():
    return lax.rem(lax.axis_index("row"), 2)


def join_kernel(first, second, pair):
    inner = first.shape[0]
    pair[:inner, :] = first[...]
    pair[inner:, :] = second[...]


def split(value):
    high = value.astype(BF16)
    low = (value - high.astype(F32)).astype(BF16)
    return high, low


dot = functools.partial(jnp.dot, preferred_element_type=F32)


def product(left_high, left_low, right_high, right_low):
    return dot(left_high, right_high) + (dot(left_high, right_low) + dot(left_low, right_high))


def take_left(index, block, left_high, left_low):
    rows = pl.ds(index * TILE, TILE)
    high, low = split(block[...].T)
    left_high[rows, :] = high
    left_low[rows, :] = low


def take_right(index, parity, block, right_high, right_low):
    start = 2 * index * TILE + parity * TILE
    columns = pl.ds(start if isinstance(start, int) else pl.multiple_of(start, TILE), TILE)
    high, low = split(block[...])
    right_high[:, columns] = high
    right_low[:, columns] = low


def halves(pair):
    inner = pair.shape[0] // 2
    return pair.at[pl.ds(0, inner), :], pair.at[pl.ds(inner, inner), :]


def early_product_kernel(own, other, o1, s1, o3, s3, left_high, left_low, right_high, right_low, total):
    left, right = (left_high, left_low), (right_high, right_low)
    take_left(0, own, *left)
    take_right(0, core(), own, *right)
    take_right(0, 1 - core(), other, *right)

    @pl.when(core() == 0)
    def _():
        take_left(1, o1, *left)
        take_left(2, o3, *left)
        columns = pl.ds(0, 2 * TILE)
        total[:, columns] = product(left_high[...], left_low[...], right_high[:, columns], right_low[:, columns])

    @pl.when(core() == 1)
    def _():
        for index, o, s in ((1, o1, s1), (2, o3, s3)):
            take_right(index, 0, s, *right)
            take_right(index, 1, o, *right)
        rows = pl.ds(0, TILE)
        total[rows, :] = product(left_high[rows, :], left_low[rows, :], right_high[...], right_low[...])


def first_product_kernel(o1_s3, o3_s1, early_left, early_left_low, early_right, early_right_low, *refs):
    left_high, left_low, right_high, right_low, beside, below = refs
    (o1, s3), (o3, s1) = halves(o1_s3), halves(o3_s1)

    @pl.when(core() == 0)
    def _():
        for index, o, s in ((0, o1, s1), (1, o3, s3)):
            take_right(index, 0, s, right_high, right_low)
            take_right(index, 1, o, right_high, right_low)
        beside[...] = product(early_left[...], early_left_low[...], right_high[...], right_low[...])

    @pl.when(core() == 1)
    def _():
        take_left(0, s1, left_high, left_low)
        take_left(1, s3, left_high, left_low)
        below[...] = product(left_high[...], left_low[...], early_right[...], early_right_low[...])


def turn():
    return 1 - 2 * core()


def strip(index):
    return pl.ds(pl.multiple_of(index * SUB, SUB), SUB)


def scatter(total, send, keep):
    z, y = lax.axis_index("layer"), lax.axis_index("col")

    def rows_of(layer):
        t = lax.rem(layer // 4 - y + N_COL, N_COL)
        index = jnp.where(t < 2, t, 5 - t)
        return strip(index * 4 + lax.rem(layer, 4))

    for j in range(N_LAYER // 2):
        rows = pl.ds(j * SUB, SUB)
        keep[rows, :] = total[rows_of(lax.rem(z + 2 * j, N_LAYER)), :]
        send[rows, :] = total[rows_of(lax.rem(z + turn() + 2 * j + N_LAYER, N_LAYER)), :]


def second_product_kernel(o2, s2, both, early_right, early_right_low, early, right_high, right_low, beside, below, *refs):
    send, keep, last_high, last_low, total = refs
    known, wide = early.shape[0], 2 * TILE
    first, next_ = pl.ds(0, wide), pl.ds(wide, wide)

    def last_rows(columns, high, low):
        total[known:, columns] = product(last_high[...], last_low[...], high, low)

    @pl.when(core() == 0)
    def _():
        take_left(0, o2, last_high, last_low)
        total[:known, first] = early[:, first]
        total[:known, next_] = beside[:, first]
        last_rows(first, early_right[:, first], early_right_low[:, first])
        last_rows(next_, right_high[:, first], right_low[:, first])

    @pl.when(core() == 1)
    def _():
        columns = pl.ds(0, 2 * wide)
        take_left(0, both.at[pl.ds(s2.shape[0], s2.shape[0]), :], last_high, last_low)
        total[:TILE, :] = early[:TILE, columns]
        total[TILE:known, :] = below[:, columns]
        last_rows(columns, early_right[:, columns], early_right_low[:, columns])

    scatter(total, send, keep)


def third_product_kernel(o2, s2, both, last_high, last_low, *refs):
    early_left, early_left_low, early_right, early_right_low, early = refs[:5]
    left_high, left_low, right_high, right_low, beside, below = refs[5:11]
    send, keep, far_high, far_low, total = refs[11:]
    o2_swapped, s2_swapped = halves(both)
    known, wide = early.shape[0], 2 * TILE
    first, next_, third = (pl.ds(i * wide, wide) for i in range(3))

    def far(rows, high, low):
        total[rows, next_] = product(high, low, far_high[...], far_low[...])

    @pl.when(core() == 0)
    def _():
        take_right(0, 0, s2_swapped, far_high, far_low)
        take_right(0, 1, o2_swapped, far_high, far_low)
        total[:known, first] = beside[:, next_]
        total[known:, first] = product(last_high[...], last_low[...], right_high[:, next_], right_low[:, next_])
        far(pl.ds(0, known), early_left[...], early_left_low[...])
        far(pl.ds(known, TILE), last_high[...], last_low[...])

    @pl.when(core() == 1)
    def _():
        take_right(0, 0, s2, far_high, far_low)
        take_right(0, 1, o2, far_high, far_low)
        total[:TILE, first] = early[:TILE, third]
        total[TILE:known, first] = below[:, third]
        total[known:, first] = product(last_high[...], last_low[...], early_right[:, third], early_right_low[:, third])
        far(pl.ds(0, TILE), early_left[:TILE, :], early_left_low[:TILE, :])
        far(pl.ds(TILE, known - TILE), left_high[...], left_low[...])
        far(pl.ds(known, TILE), last_high[...], last_low[...])

    scatter(total, send, keep)


def stage_kernel(held, came, send, keep):
    count = held.shape[0] // SUB
    for i in range(count // 2):
        rows = pl.ds(i * SUB, SUB)
        near = pl.ds(2 * i * SUB, SUB)
        far = strip(lax.rem(turn() + 2 * i + count, count))
        keep[rows, :] = held[near, :] + came[near, :]
        send[rows, :] = held[far, :] + came[far, :]


def group_kernel(held, came, own, up, far, down):
    for i, out in enumerate((own, up, far, down)):
        rows = pl.ds(i * SUB, SUB)
        out[...] = held[rows, :] + came[rows, :]


def up_kernel(first, second, came, out):
    half = first.shape[1]
    out[:, :half] = first[...] + came[...]
    out[:, half:] = second[...]


def down_kernel(first, second, came, out):
    half = first.shape[1]
    out[:, :half] = first[...]
    out[:, half:] = second[...] + came[...]


def below_kernel(first, second, from_below, out):
    half = first.shape[1]
    out[:, :half] = first[...] + from_below[:, :half]
    out[:, half:] = second[...] + from_below[:, half:]


def last_kernel(held, from_above, out):
    x = lax.axis_index("row") // 2
    for index, t in enumerate(ORDER):
        source = pl.ds(index * 2 * TILE, 2 * TILE)
        target = pl.ds(pl.multiple_of(lax.rem(x + t, N_X) * 2 * TILE, 2 * TILE), 2 * TILE)
        out[:, target] = held[:, source] + from_above[:, source]


def swap(value):
    return lax.ppermute(value, "row", [(i, i ^ 1) for i in range(N_ROW)])


def fetch(value, t):
    pairs = []
    for x in range(N_X):
        for y in range(N_COL):
            pairs.append(((2 * x) * N_COL + (y + t) % N_COL, (2 * x) * N_COL + y))
            pairs.append(((2 * ((x + t) % N_X) + 1) * N_COL + y, (2 * x + 1) * N_COL + y))
    return lax.ppermute(value, ("row", "col"), pairs)


def fetch_across(value, t):
    pairs = []
    for x in range(N_X):
        for y in range(N_COL):
            pairs.append(((2 * x + 1) * N_COL + (y + t) % N_COL, (2 * x) * N_COL + y))
            pairs.append(((2 * ((x + t) % N_X)) * N_COL + y, (2 * x + 1) * N_COL + y))
    return lax.ppermute(value, ("row", "col"), pairs)


def pass_on(value, distance):
    pairs = []
    for z in range(N_LAYER):
        for row in range(N_ROW):
            to = (z + (distance if row % 2 == 0 else -distance)) % N_LAYER
            pairs.append((z * N_ROW + row, to * N_ROW + row))
    return lax.ppermute(value, ("layer", "row"), pairs)


def shift_layers(value, distance):
    return lax.ppermute(value, "layer", [(z, (z + distance) % N_LAYER) for z in range(N_LAYER)])


def on_device(graph, pattern):
    inner = graph.shape[0]
    tiles = inner // TILE
    (masked,) = call(
        mask_kernel,
        [(inner, TILE)],
        (graph, pattern.reshape(-1)),
        [pl.BlockSpec(memory_space=pltpu.HBM)] * 2,
        scratch=[
            pltpu.VMEM((inner, TILE), F32),
            pltpu.SMEM((tiles,), jnp.int32),
            pltpu.SemaphoreType.DMA((tiles + 1,)),
        ],
        limit=62 * 1024 * 1024,
    )
    other = swap(masked)
    o1, o3 = fetch(masked, 1), fetch(masked, 3)
    s3, s1 = fetch_across(masked, 3), fetch_across(masked, 1)
    o2, s2 = fetch(o1, 1), fetch(s3, 3)

    def swap_two(first, second, after=None):
        return swap(call(join_kernel, [(2 * inner, TILE)], (first, second), after=after)[0])

    known, wide = 3 * TILE, 6 * TILE
    shapes = [((known, inner), BF16)] * 2 + [((inner, wide), BF16)] * 2 + [(known, wide)]
    early = call(early_product_kernel, shapes, (masked, other, o1, s1, o3, s3), nbytes=1 << 10)
    second = (o2, s2, swap_two(o2, s2, after=early[4]))
    late = call(
        first_product_kernel,
        [((known - TILE, inner), BF16)] * 2
        + [((inner, wide - 2 * TILE), BF16)] * 2
        + [(known, wide - 2 * TILE), (known - TILE, wide)],
        (swap_two(o1, s3), swap_two(o3, s1), *early[:4]),
        flops=4 * known * wide * inner,
        nbytes=8 << 20,
    )
    out = (8 * SUB, 4 * TILE)
    total = pltpu.VMEM((4 * TILE, 4 * TILE), F32)
    send_a, keep_a, *last = call(
        second_product_kernel,
        [out, out, ((TILE, inner), BF16), ((TILE, inner), BF16)],
        (*second, *early[2:], *late[2:]),
        scratch=[total],
        flops=6 * TILE * 4 * TILE * inner,
        nbytes=4 << 20,
    )
    send_b, keep_b = call(
        third_product_kernel,
        [out, out],
        (*second, *last, *early, *late),
        scratch=[pltpu.VMEM((inner, 2 * TILE), BF16)] * 2 + [total],
        flops=6 * 5 * TILE * 2 * TILE * inner,
        nbytes=4 << 20,
    )
    sends, keeps = [send_a, send_b], [keep_a, keep_b]
    arrived = [pass_on(sends[half], 1) for half in range(2)]
    done = None
    for half in range(2):
        sends[half], keeps[half] = call(
            stage_kernel, [(4 * SUB, 4 * TILE)] * 2, (keeps[half], arrived[half]), after=done
        )
        done = keeps[half]
        arrived[half] = pass_on(sends[half], 2)
    first = call(group_kernel, [(SUB, 4 * TILE)] * 4, (keeps[0], arrived[0]))
    second = call(group_kernel, [(SUB, 4 * TILE)] * 4, (keeps[1], arrived[1]), after=first[0])
    chunk = [(SUB, 8 * TILE)]
    (up,) = call(up_kernel, chunk, (first[1], second[1], shift_layers(first[2], 4)))
    (down,) = call(down_kernel, chunk, (first[3], second[3], shift_layers(second[2], -4)), after=up)
    (held,) = call(below_kernel, chunk, (first[0], second[0], shift_layers(up, 4)))
    return call(last_kernel, chunk, (held, shift_layers(down, -4)))[0]


def solution(mesh):
    placed = (P("layer", ("row", "col")), P("layer", ("row", "col")))
    return jax.shard_map(
        on_device, mesh=mesh, in_specs=placed, out_specs=P(("row", "layer"), "col"), check_vma=False
    )
```

```python
import functools

import jax
import jax.numpy as jnp
from jax import lax
from jax.experimental import pallas as pl
from jax.experimental.pallas import tpu as pltpu
from jax.sharding import PartitionSpec as P

TILE = 128
N_LAYER = 16
N_X = 4
N_ROW = 8
N_COL = 4
SUB = 32
ORDER = (0, 1, 3, 2)
VMEM = pl.BlockSpec(memory_space=pltpu.VMEM)
SMEM = pl.BlockSpec(memory_space=pltpu.SMEM)
LIMIT = 40 * 1024 * 1024
F32, BF16 = jnp.float32, jnp.bfloat16


def call(kernel, outs, operands, specs=None, scratch=(), flops=0, nbytes=1 << 20, after=None, limit=LIMIT):
    if after is not None:
        inner_kernel, count = kernel, len(operands)
        kernel = lambda *refs: inner_kernel(*refs[:count], *refs[count + 1 :])
        specs = [VMEM] * count + [pl.BlockSpec(memory_space=pl.ANY)]
        operands = (*operands, after)
    outs = [o if isinstance(o[0], tuple) else (o, F32) for o in outs]
    return pl.pallas_call(
        kernel,
        out_shape=tuple(jax.ShapeDtypeStruct(s, d) for s, d in outs),
        in_specs=specs or [VMEM] * len(operands),
        out_specs=tuple(VMEM for _ in outs),
        scratch_shapes=list(scratch),
        compiler_params=pltpu.CompilerParams(vmem_limit_bytes=limit),
        cost_estimate=pl.CostEstimate(flops=flops, bytes_accessed=nbytes, transcendentals=0),
    )(*operands)


def mask_kernel(graph, pattern, masked, raw, flags, sems):
    tiles = graph.shape[0] // TILE
    flag_copy = pltpu.make_async_copy(pattern, flags, sems.at[tiles])
    flag_copy.start()
    copies = []
    for k in range(tiles):
        rows = pl.ds(k * TILE, TILE)
        copies.append(pltpu.make_async_copy(graph.at[rows, :], raw.at[rows, :], sems.at[k]))
        copies[k].start()
    flag_copy.wait()
    for k in range(tiles):
        rows = pl.ds(k * TILE, TILE)
        copies[k].wait()
        masked[rows, :] = raw[rows, :] * flags[k].astype(F32)


def core():
    return lax.rem(lax.axis_index("row"), 2)


def join_kernel(first, second, pair):
    inner = first.shape[0]
    pair[:inner, :] = first[...]
    pair[inner:, :] = second[...]


def split(value):
    high = value.astype(BF16)
    low = (value - high.astype(F32)).astype(BF16)
    return high, low


dot = functools.partial(jnp.dot, preferred_element_type=F32)


def product(left_high, left_low, right_high, right_low):
    return dot(left_high, right_high) + (dot(left_high, right_low) + dot(left_low, right_high))


def take_left(index, block, left_high, left_low):
    rows = pl.ds(index * TILE, TILE)
    high, low = split(block[...].T)
    left_high[rows, :] = high
    left_low[rows, :] = low


def take_right(index, parity, block, right_high, right_low):
    start = 2 * index * TILE + parity * TILE
    columns = pl.ds(start if isinstance(start, int) else pl.multiple_of(start, TILE), TILE)
    high, low = split(block[...])
    right_high[:, columns] = high
    right_low[:, columns] = low


def halves(pair):
    inner = pair.shape[0] // 2
    return pair.at[pl.ds(0, inner), :], pair.at[pl.ds(inner, inner), :]


def early_product_kernel(own, other, o1, s1, o3, s3, left_high, left_low, right_high, right_low, total):
    left, right = (left_high, left_low), (right_high, right_low)
    take_left(0, own, *left)
    take_right(0, core(), own, *right)
    take_right(0, 1 - core(), other, *right)

    @pl.when(core() == 0)
    def _():
        take_left(1, o1, *left)
        take_left(2, o3, *left)
        columns = pl.ds(0, 2 * TILE)
        total[:, columns] = product(left_high[...], left_low[...], right_high[:, columns], right_low[:, columns])

    @pl.when(core() == 1)
    def _():
        for index, o, s in ((1, o1, s1), (2, o3, s3)):
            take_right(index, 0, s, *right)
            take_right(index, 1, o, *right)
        rows = pl.ds(0, TILE)
        total[rows, :] = product(left_high[rows, :], left_low[rows, :], right_high[...], right_low[...])


def first_product_kernel(o1_s3, o3_s1, early_left, early_left_low, early_right, early_right_low, *refs):
    left_high, left_low, right_high, right_low, beside, below = refs
    (o1, s3), (o3, s1) = halves(o1_s3), halves(o3_s1)

    @pl.when(core() == 0)
    def _():
        for index, o, s in ((0, o1, s1), (1, o3, s3)):
            take_right(index, 0, s, right_high, right_low)
            take_right(index, 1, o, right_high, right_low)
        beside[...] = product(early_left[...], early_left_low[...], right_high[...], right_low[...])

    @pl.when(core() == 1)
    def _():
        take_left(0, s1, left_high, left_low)
        take_left(1, s3, left_high, left_low)
        below[...] = product(left_high[...], left_low[...], early_right[...], early_right_low[...])


def turn():
    return 1 - 2 * core()


def strip(index):
    return pl.ds(pl.multiple_of(index * SUB, SUB), SUB)


def scatter(total, outs):
    z = lax.axis_index("layer")
    for shift, out in zip((0, 1, -1, 2), outs):
        s = lax.rem(z + turn() * shift + 4, 4)
        for index in range(4):
            out[pl.ds(index * SUB, SUB), :] = total[strip(index * 4 + s), :]


def second_product_kernel(o2, s2, both, early_right, early_right_low, early, right_high, right_low, beside, below, *refs):
    outs, (last_high, last_low, total) = refs[:4], refs[4:]
    known, wide = early.shape[0], 2 * TILE
    first, next_ = pl.ds(0, wide), pl.ds(wide, wide)

    def last_rows(columns, high, low):
        total[known:, columns] = product(last_high[...], last_low[...], high, low)

    @pl.when(core() == 0)
    def _():
        take_left(0, o2, last_high, last_low)
        total[:known, first] = early[:, first]
        total[:known, next_] = beside[:, first]
        last_rows(first, early_right[:, first], early_right_low[:, first])
        last_rows(next_, right_high[:, first], right_low[:, first])

    @pl.when(core() == 1)
    def _():
        columns = pl.ds(0, 2 * wide)
        take_left(0, both.at[pl.ds(s2.shape[0], s2.shape[0]), :], last_high, last_low)
        total[:TILE, :] = early[:TILE, columns]
        total[TILE:known, :] = below[:, columns]
        last_rows(columns, early_right[:, columns], early_right_low[:, columns])

    scatter(total, outs)


def third_product_kernel(o2, s2, both, last_high, last_low, *refs):
    early_left, early_left_low, early_right, early_right_low, early = refs[:5]
    left_high, left_low, right_high, right_low, beside, below = refs[5:11]
    outs, (far_high, far_low, total) = refs[11:15], refs[15:]
    o2_swapped, s2_swapped = halves(both)
    known, wide = early.shape[0], 2 * TILE
    first, next_, third = (pl.ds(i * wide, wide) for i in range(3))

    def far(rows, high, low):
        total[rows, next_] = product(high, low, far_high[...], far_low[...])

    @pl.when(core() == 0)
    def _():
        take_right(0, 0, s2_swapped, far_high, far_low)
        take_right(0, 1, o2_swapped, far_high, far_low)
        total[:known, first] = beside[:, next_]
        total[known:, first] = product(last_high[...], last_low[...], right_high[:, next_], right_low[:, next_])
        far(pl.ds(0, known), early_left[...], early_left_low[...])
        far(pl.ds(known, TILE), last_high[...], last_low[...])

    @pl.when(core() == 1)
    def _():
        take_right(0, 0, s2, far_high, far_low)
        take_right(0, 1, o2, far_high, far_low)
        total[:TILE, first] = early[:TILE, third]
        total[TILE:known, first] = below[:, third]
        total[known:, first] = product(last_high[...], last_low[...], early_right[:, third], early_right_low[:, third])
        far(pl.ds(0, TILE), early_left[:TILE, :], early_left_low[:TILE, :])
        far(pl.ds(TILE, known - TILE), left_high[...], left_low[...])
        far(pl.ds(known, TILE), last_high[...], last_low[...])

    scatter(total, outs)


def add_kernel(held, came, out):
    out[...] = held[...] + came[...]


def group_kernel(mine, below, above, own, up, far, down):
    group, y = lax.axis_index("layer") // 4, lax.axis_index("col")
    for i, out in enumerate((own, up, far, down)):
        t = lax.rem(group + turn() * i - y + 8, 4)
        rows = strip(jnp.where(t < 2, t, 5 - t))
        out[...] = mine[rows, :] + (below[rows, :] + above[rows, :])


def up_kernel(first, second, came, out):
    half = first.shape[1]
    out[:, :half] = first[...] + came[...]
    out[:, half:] = second[...]


def down_kernel(first, second, came, out):
    half = first.shape[1]
    out[:, :half] = first[...]
    out[:, half:] = second[...] + came[...]


def below_kernel(first, second, from_below, out):
    half = first.shape[1]
    out[:, :half] = first[...] + from_below[:, :half]
    out[:, half:] = second[...] + from_below[:, half:]


def last_kernel(held, from_above, out):
    x = lax.axis_index("row") // 2
    for index, t in enumerate(ORDER):
        source = pl.ds(index * 2 * TILE, 2 * TILE)
        target = pl.ds(pl.multiple_of(lax.rem(x + t, N_X) * 2 * TILE, 2 * TILE), 2 * TILE)
        out[:, target] = held[:, source] + from_above[:, source]


def swap(value):
    return lax.ppermute(value, "row", [(i, i ^ 1) for i in range(N_ROW)])


def fetch(value, t):
    pairs = []
    for x in range(N_X):
        for y in range(N_COL):
            pairs.append(((2 * x) * N_COL + (y + t) % N_COL, (2 * x) * N_COL + y))
            pairs.append(((2 * ((x + t) % N_X) + 1) * N_COL + y, (2 * x + 1) * N_COL + y))
    return lax.ppermute(value, ("row", "col"), pairs)


def pass_on(value, distance):
    pairs = []
    for z in range(N_LAYER):
        for row in range(N_ROW):
            to = (z + (distance if row % 2 == 0 else -distance)) % N_LAYER
            pairs.append((z * N_ROW + row, to * N_ROW + row))
    return lax.ppermute(value, ("layer", "row"), pairs)


def on_device(graph, pattern):
    inner = graph.shape[0]
    tiles = inner // TILE
    (masked,) = call(
        mask_kernel,
        [(inner, TILE)],
        (graph, pattern.reshape(-1)),
        [pl.BlockSpec(memory_space=pltpu.HBM)] * 2,
        scratch=[
            pltpu.VMEM((inner, TILE), F32),
            pltpu.SMEM((tiles,), jnp.int32),
            pltpu.SemaphoreType.DMA((tiles + 1,)),
        ],
        limit=62 * 1024 * 1024,
    )
    other = swap(masked)
    o1, o3 = fetch(masked, 1), fetch(masked, 3)
    s3, s1 = fetch(other, 3), fetch(other, 1)
    o2, s2 = fetch(o1, 1), fetch(s3, 3)

    def swap_two(first, second, after=None):
        return swap(call(join_kernel, [(2 * inner, TILE)], (first, second), after=after)[0])

    known, wide = 3 * TILE, 6 * TILE
    shapes = [((known, inner), BF16)] * 2 + [((inner, wide), BF16)] * 2 + [(known, wide)]
    early = call(early_product_kernel, shapes, (masked, other, o1, s1, o3, s3), nbytes=1 << 10)
    second = (o2, s2, swap_two(o2, s2, after=early[4]))
    late = call(
        first_product_kernel,
        [((known - TILE, inner), BF16)] * 2
        + [((inner, wide - 2 * TILE), BF16)] * 2
        + [(known, wide - 2 * TILE), (known - TILE, wide)],
        (swap_two(o1, s3), swap_two(o3, s1), *early[:4]),
        flops=4 * known * wide * inner,
        nbytes=8 << 20,
    )
    cut = (4 * SUB, 4 * TILE)
    total = pltpu.VMEM((4 * TILE, 4 * TILE), F32)
    mine_a, up_a, down_a, two_a, *last = call(
        second_product_kernel,
        [cut] * 4 + [((TILE, inner), BF16)] * 2,
        (*second, *early[2:], *late[2:]),
        scratch=[total],
        flops=6 * TILE * 4 * TILE * inner,
        nbytes=4 << 20,
    )
    mine_b, up_b, down_b, two_b = call(
        third_product_kernel,
        [cut] * 4,
        (*second, *last, *early, *late),
        scratch=[pltpu.VMEM((inner, 2 * TILE), BF16)] * 2 + [total],
        flops=6 * 5 * TILE * 2 * TILE * inner,
        nbytes=4 << 20,
    )
    (up_a,) = call(add_kernel, [cut], (up_a, pass_on(two_a, 1)))
    (down_b,) = call(add_kernel, [cut], (down_b, pass_on(two_b, -1)), after=up_a)
    piece = [(SUB, 4 * TILE)] * 4
    first = call(group_kernel, piece, (mine_a, pass_on(up_a, 1), pass_on(down_a, -1)))
    second = call(
        group_kernel, piece, (mine_b, pass_on(up_b, 1), pass_on(down_b, -1)), after=first[0]
    )
    chunk = [(SUB, 8 * TILE)]
    (up,) = call(up_kernel, chunk, (first[1], second[1], pass_on(first[2], 4)))
    (down,) = call(down_kernel, chunk, (first[3], second[3], pass_on(second[2], -4)), after=up)
    (held,) = call(below_kernel, chunk, (first[0], second[0], pass_on(up, 4)))
    return call(last_kernel, chunk, (held, pass_on(down, -4)))[0]


def solution(mesh):
    placed = (P("layer", ("row", "col")), P("layer", ("row", "col")))
    return jax.shard_map(
        on_device, mesh=mesh, in_specs=placed, out_specs=P(("row", "layer"), "col"), check_vma=False
    )
```

```python
import functools

import jax
import jax.numpy as jnp
from jax import lax
from jax.experimental import pallas as pl
from jax.experimental.pallas import tpu as pltpu
from jax.sharding import PartitionSpec as P

TILE = 128
N_LAYER = 16
N_X = 4
N_ROW = 8
N_COL = 4
SUB = 32
ORDER = (0, 1, 3, 2)
VMEM = pl.BlockSpec(memory_space=pltpu.VMEM)
SMEM = pl.BlockSpec(memory_space=pltpu.SMEM)
LIMIT = 40 * 1024 * 1024
F32, BF16 = jnp.float32, jnp.bfloat16


def call(kernel, outs, operands, specs=None, scratch=(), flops=0, nbytes=1 << 20, after=None, limit=LIMIT, out_spec=VMEM):
    if after is not None:
        inner_kernel, count = kernel, len(operands)
        kernel = lambda *refs: inner_kernel(*refs[:count], *refs[count + 1 :])
        specs = [VMEM] * count + [pl.BlockSpec(memory_space=pl.ANY)]
        operands = (*operands, after)
    outs = [o if isinstance(o[0], tuple) else (o, F32) for o in outs]
    return pl.pallas_call(
        kernel,
        out_shape=tuple(jax.ShapeDtypeStruct(s, d) for s, d in outs),
        in_specs=specs or [VMEM] * len(operands),
        out_specs=tuple(out_spec for _ in outs),
        scratch_shapes=list(scratch),
        compiler_params=pltpu.CompilerParams(vmem_limit_bytes=limit),
        cost_estimate=pl.CostEstimate(flops=flops, bytes_accessed=nbytes, transcendentals=0),
    )(*operands)


def mask_kernel(graph, pattern, masked, raw, flags, sems, out_sems):
    tiles = graph.shape[0] // TILE
    flag_copy = pltpu.make_async_copy(pattern, flags, sems.at[tiles])
    flag_copy.start()
    copies, outs = [], []
    for k in range(tiles):
        rows = pl.ds(k * TILE, TILE)
        copies.append(pltpu.make_async_copy(graph.at[rows, :], raw.at[rows, :], sems.at[k]))
        outs.append(pltpu.make_async_copy(raw.at[rows, :], masked.at[rows, :], out_sems.at[k]))
        copies[k].start()
    flag_copy.wait()
    for k in range(tiles):
        rows = pl.ds(k * TILE, TILE)
        copies[k].wait()
        raw[rows, :] = raw[rows, :] * flags[k].astype(F32)
        outs[k].start()
    for out in outs:
        out.wait()


def core():
    return lax.rem(lax.axis_index("row"), 2)


def join_kernel(first, second, pair):
    rows = first.shape[0]
    pair[:rows, :] = first[...]
    pair[rows:, :] = second[...]


def split(value):
    high = value.astype(BF16)
    low = (value - high.astype(F32)).astype(BF16)
    return high, low


dot = functools.partial(jnp.dot, preferred_element_type=F32)


def product(left_high, left_low, right_high, right_low):
    return dot(left_high, right_high) + (dot(left_high, right_low) + dot(left_low, right_high))


def take_left(index, block, left_high, left_low):
    rows = pl.ds(index * TILE, TILE)
    high, low = split(block[...].T)
    left_high[rows, :] = high
    left_low[rows, :] = low


def take_right(index, parity, block, right_high, right_low):
    start = 2 * index * TILE + parity * TILE
    columns = pl.ds(start if isinstance(start, int) else pl.multiple_of(start, TILE), TILE)
    high, low = split(block[...])
    right_high[:, columns] = high
    right_low[:, columns] = low


def halves(pair):
    inner = pair.shape[0] // 2
    return pair.at[pl.ds(0, inner), :], pair.at[pl.ds(inner, inner), :]


def early_product_kernel(own, other, o1, s1, o3, s3, left_high, left_low, right_high, right_low, total):
    left, right = (left_high, left_low), (right_high, right_low)
    take_left(0, own, *left)
    take_right(0, core(), own, *right)
    take_right(0, 1 - core(), other, *right)

    @pl.when(core() == 0)
    def _():
        take_left(1, o1, *left)
        take_left(2, o3, *left)
        columns = pl.ds(0, 2 * TILE)
        total[:, columns] = product(left_high[...], left_low[...], right_high[:, columns], right_low[:, columns])

    @pl.when(core() == 1)
    def _():
        for index, o, s in ((1, o1, s1), (2, o3, s3)):
            take_right(index, 0, s, *right)
            take_right(index, 1, o, *right)
        rows = pl.ds(0, TILE)
        total[rows, :] = product(left_high[rows, :], left_low[rows, :], right_high[...], right_low[...])


def first_product_kernel(o1_s3, o3_s1, early_left, early_left_low, early_right, early_right_low, *refs):
    left_high, left_low, right_high, right_low, beside, below = refs
    (o1, s3), (o3, s1) = halves(o1_s3), halves(o3_s1)

    @pl.when(core() == 0)
    def _():
        for index, o, s in ((0, o1, s1), (1, o3, s3)):
            take_right(index, 0, s, right_high, right_low)
            take_right(index, 1, o, right_high, right_low)
        beside[...] = product(early_left[...], early_left_low[...], right_high[...], right_low[...])

    @pl.when(core() == 1)
    def _():
        take_left(0, s1, left_high, left_low)
        take_left(1, s3, left_high, left_low)
        below[...] = product(left_high[...], left_low[...], early_right[...], early_right_low[...])


def turn():
    return 1 - 2 * core()


def strip(index):
    return pl.ds(pl.multiple_of(index * SUB, SUB), SUB)


def scatter(total, outs):
    z = lax.axis_index("layer")
    for shift, out in zip((0, 1, -1, 2), outs):
        s = lax.rem(z + turn() * shift + 4, 4)
        for index in range(4):
            out[pl.ds(index * SUB, SUB), :] = total[strip(index * 4 + s), :]


def second_product_kernel(o2, s2, both, early_right, early_right_low, early, right_high, right_low, beside, below, *refs):
    outs, (last_high, last_low, total) = refs[:4], refs[4:]
    known, wide = early.shape[0], 2 * TILE
    first, next_ = pl.ds(0, wide), pl.ds(wide, wide)

    def last_rows(columns, high, low):
        total[known:, columns] = product(last_high[...], last_low[...], high, low)

    @pl.when(core() == 0)
    def _():
        take_left(0, o2, last_high, last_low)
        total[:known, first] = early[:, first]
        total[:known, next_] = beside[:, first]
        last_rows(first, early_right[:, first], early_right_low[:, first])
        last_rows(next_, right_high[:, first], right_low[:, first])

    @pl.when(core() == 1)
    def _():
        columns = pl.ds(0, 2 * wide)
        take_left(0, both.at[pl.ds(s2.shape[0], s2.shape[0]), :], last_high, last_low)
        total[:TILE, :] = early[:TILE, columns]
        total[TILE:known, :] = below[:, columns]
        last_rows(columns, early_right[:, columns], early_right_low[:, columns])

    scatter(total, outs)


def third_product_kernel(o2, s2, both, last_high, last_low, *refs):
    early_left, early_left_low, early_right, early_right_low, early = refs[:5]
    left_high, left_low, right_high, right_low, beside, below = refs[5:11]
    outs, (far_high, far_low, total) = refs[11:15], refs[15:]
    o2_swapped, s2_swapped = halves(both)
    known, wide = early.shape[0], 2 * TILE
    first, next_, third = (pl.ds(i * wide, wide) for i in range(3))

    def far(rows, high, low):
        total[rows, next_] = product(high, low, far_high[...], far_low[...])

    @pl.when(core() == 0)
    def _():
        take_right(0, 0, s2_swapped, far_high, far_low)
        take_right(0, 1, o2_swapped, far_high, far_low)
        total[:known, first] = beside[:, next_]
        total[known:, first] = product(last_high[...], last_low[...], right_high[:, next_], right_low[:, next_])
        far(pl.ds(0, known), early_left[...], early_left_low[...])
        far(pl.ds(known, TILE), last_high[...], last_low[...])

    @pl.when(core() == 1)
    def _():
        take_right(0, 0, s2, far_high, far_low)
        take_right(0, 1, o2, far_high, far_low)
        total[:TILE, first] = early[:TILE, third]
        total[TILE:known, first] = below[:, third]
        total[known:, first] = product(last_high[...], last_low[...], early_right[:, third], early_right_low[:, third])
        far(pl.ds(0, TILE), early_left[:TILE, :], early_left_low[:TILE, :])
        far(pl.ds(TILE, known - TILE), left_high[...], left_low[...])
        far(pl.ds(known, TILE), last_high[...], last_low[...])

    scatter(total, outs)


def add_kernel(held, came, out):
    out[...] = held[...] + came[...]


def group_kernel(half, mine, below, both_above, own, up, far, down):
    group, y = lax.axis_index("layer") // 4, lax.axis_index("col")
    above = both_above.at[pl.ds(half * mine.shape[0], mine.shape[0]), :]
    for i, out in enumerate((own, up, far, down)):
        t = lax.rem(group + turn() * i - y + 8, 4)
        rows = strip(jnp.where(t < 2, t, 5 - t))
        out[...] = mine[rows, :] + (below[rows, :] + above[rows, :])


def up_kernel(first, second, came, out):
    half = first.shape[1]
    out[:, :half] = first[...] + came[...]
    out[:, half:] = second[...]


def down_kernel(first, second, came, out):
    half = first.shape[1]
    out[:, :half] = first[...]
    out[:, half:] = second[...] + came[...]


def below_kernel(first, second, from_below, out):
    half = first.shape[1]
    out[:, :half] = first[...] + from_below[:, :half]
    out[:, half:] = second[...] + from_below[:, half:]


def last_kernel(held, from_above, out):
    x = lax.axis_index("row") // 2
    for index, t in enumerate(ORDER):
        source = pl.ds(index * 2 * TILE, 2 * TILE)
        target = pl.ds(pl.multiple_of(lax.rem(x + t, N_X) * 2 * TILE, 2 * TILE), 2 * TILE)
        out[:, target] = held[:, source] + from_above[:, source]


def swap(value):
    return lax.ppermute(value, "row", [(i, i ^ 1) for i in range(N_ROW)])


def fetch(value, t):
    pairs = []
    for x in range(N_X):
        for y in range(N_COL):
            pairs.append(((2 * x) * N_COL + (y + t) % N_COL, (2 * x) * N_COL + y))
            pairs.append(((2 * ((x + t) % N_X) + 1) * N_COL + y, (2 * x + 1) * N_COL + y))
    return lax.ppermute(value, ("row", "col"), pairs)


def pass_on(value, distance):
    pairs = []
    for z in range(N_LAYER):
        for row in range(N_ROW):
            to = (z + (distance if row % 2 == 0 else -distance)) % N_LAYER
            pairs.append((z * N_ROW + row, to * N_ROW + row))
    return lax.ppermute(value, ("layer", "row"), pairs)


def on_device(graph, pattern):
    inner = graph.shape[0]
    tiles = inner // TILE
    (masked,) = call(
        mask_kernel,
        [(inner, TILE)],
        (graph, pattern.reshape(-1)),
        [pl.BlockSpec(memory_space=pltpu.HBM)] * 2,
        scratch=[
            pltpu.VMEM((inner, TILE), F32),
            pltpu.SMEM((tiles,), jnp.int32),
            pltpu.SemaphoreType.DMA((tiles + 1,)),
            pltpu.SemaphoreType.DMA((tiles,)),
        ],
        limit=62 * 1024 * 1024,
        out_spec=pl.BlockSpec(memory_space=pltpu.HBM),
    )
    other = swap(masked)
    o1, o3 = fetch(masked, 1), fetch(masked, 3)
    s3, s1 = fetch(other, 3), fetch(other, 1)
    o2, s2 = fetch(o1, 1), fetch(s3, 3)

    def swap_two(first, second, after=None):
        return swap(call(join_kernel, [(2 * inner, TILE)], (first, second), after=after)[0])

    known, wide = 3 * TILE, 6 * TILE
    shapes = [((known, inner), BF16)] * 2 + [((inner, wide), BF16)] * 2 + [(known, wide)]
    early = call(early_product_kernel, shapes, (masked, other, o1, s1, o3, s3), nbytes=1 << 10)
    second = (o2, s2, swap_two(o2, s2, after=early[4]))
    late = call(
        first_product_kernel,
        [((known - TILE, inner), BF16)] * 2
        + [((inner, wide - 2 * TILE), BF16)] * 2
        + [(known, wide - 2 * TILE), (known - TILE, wide)],
        (swap_two(o1, s3), swap_two(o3, s1), *early[:4]),
        flops=4 * known * wide * inner,
        nbytes=8 << 20,
    )
    cut = (4 * SUB, 4 * TILE)
    total = pltpu.VMEM((4 * TILE, 4 * TILE), F32)
    mine_a, up_a, down_a, two_a, *last = call(
        second_product_kernel,
        [cut] * 4 + [((TILE, inner), BF16)] * 2,
        (*second, *early[2:], *late[2:]),
        scratch=[total],
        flops=6 * TILE * 4 * TILE * inner,
        nbytes=4 << 20,
    )
    mine_b, up_b, down_b, two_b = call(
        third_product_kernel,
        [cut] * 4,
        (*second, *last, *early, *late),
        scratch=[pltpu.VMEM((inner, 2 * TILE), BF16)] * 2 + [total],
        flops=6 * 5 * TILE * 2 * TILE * inner,
        nbytes=4 << 20,
    )
    (downs,) = call(join_kernel, [(8 * SUB, 4 * TILE)], (down_a, down_b))
    above = pass_on(downs, -1)
    (up_a,) = call(add_kernel, [cut], (up_a, pass_on(two_a, 1)))
    (up_b,) = call(add_kernel, [cut], (up_b, pass_on(two_b, 1)), after=up_a)
    piece = [(SUB, 4 * TILE)] * 4
    first = call(functools.partial(group_kernel, 0), piece, (mine_a, pass_on(up_a, 1), above))
    second = call(functools.partial(group_kernel, 1), piece, (mine_b, pass_on(up_b, 1), above), after=first[0])
    chunk = [(SUB, 8 * TILE)]
    (up,) = call(up_kernel, chunk, (first[1], second[1], pass_on(first[2], 4)))
    (down,) = call(down_kernel, chunk, (first[3], second[3], pass_on(second[2], -4)), after=up)
    (held,) = call(below_kernel, chunk, (first[0], second[0], pass_on(up, 4)))
    return call(last_kernel, chunk, (held, pass_on(down, -4)))[0]


def solution(mesh):
    placed = (P("layer", ("row", "col")), P("layer", ("row", "col")))
    return jax.shard_map(
        on_device, mesh=mesh, in_specs=placed, out_specs=P(("row", "layer"), "col"), check_vma=False
    )
```

```python
import functools

import jax
import jax.numpy as jnp
from jax import lax
from jax.experimental import pallas as pl
from jax.experimental.pallas import tpu as pltpu
from jax.sharding import PartitionSpec as P

TILE = 128
N_LAYER = 16
N_X = 4
N_ROW = 8
N_COL = 4
SUB = 32
ORDER = (0, 1, 3, 2)
VMEM = pl.BlockSpec(memory_space=pltpu.VMEM)
SMEM = pl.BlockSpec(memory_space=pltpu.SMEM)
LIMIT = 40 * 1024 * 1024
F32, BF16 = jnp.float32, jnp.bfloat16


def call(kernel, outs, operands, specs=None, scratch=(), flops=0, nbytes=1 << 20, after=None, limit=LIMIT, out_spec=VMEM):
    if after is not None:
        inner_kernel, count = kernel, len(operands)
        kernel = lambda *refs: inner_kernel(*refs[:count], *refs[count + 1 :])
        specs = [VMEM] * count + [pl.BlockSpec(memory_space=pl.ANY)]
        operands = (*operands, after)
    outs = [o if isinstance(o[0], tuple) else (o, F32) for o in outs]
    return pl.pallas_call(
        kernel,
        out_shape=tuple(jax.ShapeDtypeStruct(s, d) for s, d in outs),
        in_specs=specs or [VMEM] * len(operands),
        out_specs=tuple(out_spec for _ in outs),
        scratch_shapes=list(scratch),
        compiler_params=pltpu.CompilerParams(vmem_limit_bytes=limit),
        cost_estimate=pl.CostEstimate(flops=flops, bytes_accessed=nbytes, transcendentals=0),
    )(*operands)


def mask_kernel(graph, pattern, masked, raw, flags, sems, out_sems):
    tiles = graph.shape[0] // TILE
    flag_copy = pltpu.make_async_copy(pattern, flags, sems.at[tiles])
    flag_copy.start()
    copies, outs = [], []
    for k in range(tiles):
        rows = pl.ds(k * TILE, TILE)
        copies.append(pltpu.make_async_copy(graph.at[rows, :], raw.at[rows, :], sems.at[k]))
        outs.append(pltpu.make_async_copy(raw.at[rows, :], masked.at[rows, :], out_sems.at[k]))
        copies[k].start()
    flag_copy.wait()
    for k in range(tiles):
        rows = pl.ds(k * TILE, TILE)
        copies[k].wait()
        raw[rows, :] = raw[rows, :] * flags[k].astype(F32)
        outs[k].start()
    for out in outs:
        out.wait()


def core():
    return lax.rem(lax.axis_index("row"), 2)


def join_kernel(first, second, pair):
    rows = first.shape[0]
    pair[:rows, :] = first[...]
    pair[rows:, :] = second[...]


def split(value):
    high = value.astype(BF16)
    low = (value - high.astype(F32)).astype(BF16)
    return high, low


dot = functools.partial(jnp.dot, preferred_element_type=F32)


def product(left_high, left_low, right_high, right_low):
    return dot(left_high, right_high) + (dot(left_high, right_low) + dot(left_low, right_high))


def take_left(index, block, left_high, left_low):
    rows = pl.ds(index * TILE, TILE)
    high, low = split(block[...].T)
    left_high[rows, :] = high
    left_low[rows, :] = low


def take_right(index, parity, block, right_high, right_low):
    start = 2 * index * TILE + parity * TILE
    columns = pl.ds(start if isinstance(start, int) else pl.multiple_of(start, TILE), TILE)
    high, low = split(block[...])
    right_high[:, columns] = high
    right_low[:, columns] = low


def halves(pair):
    inner = pair.shape[0] // 2
    return pair.at[pl.ds(0, inner), :], pair.at[pl.ds(inner, inner), :]


def early_product_kernel(own, other, o1, s1, o3, s3, left_high, left_low, right_high, right_low, total):
    left, right = (left_high, left_low), (right_high, right_low)
    take_left(0, own, *left)
    take_right(0, core(), own, *right)
    take_right(0, 1 - core(), other, *right)

    @pl.when(core() == 0)
    def _():
        take_left(1, o1, *left)
        take_left(2, o3, *left)
        columns = pl.ds(0, 2 * TILE)
        total[:, columns] = product(left_high[...], left_low[...], right_high[:, columns], right_low[:, columns])

    @pl.when(core() == 1)
    def _():
        for index, o, s in ((1, o1, s1), (2, o3, s3)):
            take_right(index, 0, s, *right)
            take_right(index, 1, o, *right)
        rows = pl.ds(0, TILE)
        total[rows, :] = product(left_high[rows, :], left_low[rows, :], right_high[...], right_low[...])


def first_product_kernel(o1_s3, o3_s1, early_left, early_left_low, early_right, early_right_low, *refs):
    left_high, left_low, right_high, right_low, beside, below = refs
    (o1, s3), (o3, s1) = halves(o1_s3), halves(o3_s1)

    @pl.when(core() == 0)
    def _():
        for index, o, s in ((0, o1, s1), (1, o3, s3)):
            take_right(index, 0, s, right_high, right_low)
            take_right(index, 1, o, right_high, right_low)
        beside[...] = product(early_left[...], early_left_low[...], right_high[...], right_low[...])

    @pl.when(core() == 1)
    def _():
        take_left(0, s1, left_high, left_low)
        take_left(1, s3, left_high, left_low)
        below[...] = product(left_high[...], left_low[...], early_right[...], early_right_low[...])


def turn():
    return 1 - 2 * core()


def strip(index):
    return pl.ds(pl.multiple_of(index * SUB, SUB), SUB)


def scatter(total, outs):
    z = lax.axis_index("layer")
    for shift, out in zip((0, 1, -1, 2), outs):
        s = lax.rem(z + turn() * shift + 4, 4)
        for index in range(4):
            out[pl.ds(index * SUB, SUB), :] = total[strip(index * 4 + s), :]


def second_product_kernel(o2, s2, both, early_right, early_right_low, early, right_high, right_low, beside, below, *refs):
    outs, (last_high, last_low, total) = refs[:4], refs[4:]
    known, wide = early.shape[0], 2 * TILE
    first, next_ = pl.ds(0, wide), pl.ds(wide, wide)

    def last_rows(columns, high, low):
        total[known:, columns] = product(last_high[...], last_low[...], high, low)

    @pl.when(core() == 0)
    def _():
        take_left(0, o2, last_high, last_low)
        total[:known, first] = early[:, first]
        total[:known, next_] = beside[:, first]
        last_rows(first, early_right[:, first], early_right_low[:, first])
        last_rows(next_, right_high[:, first], right_low[:, first])

    @pl.when(core() == 1)
    def _():
        columns = pl.ds(0, 2 * wide)
        take_left(0, both.at[pl.ds(s2.shape[0], s2.shape[0]), :], last_high, last_low)
        total[:TILE, :] = early[:TILE, columns]
        total[TILE:known, :] = below[:, columns]
        last_rows(columns, early_right[:, columns], early_right_low[:, columns])

    scatter(total, outs)


def third_product_kernel(o2, s2, both, last_high, last_low, *refs):
    early_left, early_left_low, early_right, early_right_low, early = refs[:5]
    left_high, left_low, right_high, right_low, beside, below = refs[5:11]
    outs, (far_high, far_low, total) = refs[11:15], refs[15:]
    o2_swapped, s2_swapped = halves(both)
    known, wide = early.shape[0], 2 * TILE
    first, next_, third = (pl.ds(i * wide, wide) for i in range(3))

    def far(rows, high, low):
        total[rows, next_] = product(high, low, far_high[...], far_low[...])

    @pl.when(core() == 0)
    def _():
        take_right(0, 0, s2_swapped, far_high, far_low)
        take_right(0, 1, o2_swapped, far_high, far_low)
        total[:known, first] = beside[:, next_]
        total[known:, first] = product(last_high[...], last_low[...], right_high[:, next_], right_low[:, next_])
        far(pl.ds(0, known), early_left[...], early_left_low[...])
        far(pl.ds(known, TILE), last_high[...], last_low[...])

    @pl.when(core() == 1)
    def _():
        take_right(0, 0, s2, far_high, far_low)
        take_right(0, 1, o2, far_high, far_low)
        total[:TILE, first] = early[:TILE, third]
        total[TILE:known, first] = below[:, third]
        total[known:, first] = product(last_high[...], last_low[...], early_right[:, third], early_right_low[:, third])
        far(pl.ds(0, TILE), early_left[:TILE, :], early_left_low[:TILE, :])
        far(pl.ds(TILE, known - TILE), left_high[...], left_low[...])
        far(pl.ds(known, TILE), last_high[...], last_low[...])

    scatter(total, outs)


def add_kernel(held, came, out):
    out[...] = held[...] + came[...]


def group_kernel(half, mine, below, both_above, own, up, far, down):
    group, y = lax.axis_index("layer") // 4, lax.axis_index("col")
    above = both_above.at[pl.ds(half * mine.shape[0], mine.shape[0]), :]
    for i, out in enumerate((own, up, far, down)):
        t = lax.rem(group + turn() * i - y + 8, 4)
        rows = strip(jnp.where(t < 2, t, 5 - t))
        out[...] = mine[rows, :] + (below[rows, :] + above[rows, :])


def up_kernel(first, first_came, second, second_came, out):
    half = first.shape[1]
    out[:, :half] = first[...] + first_came[...]
    out[:, half:] = second[...] + second_came[...]


def beside_kernel(first, second, out):
    half = first.shape[1]
    out[:, :half] = first[...]
    out[:, half:] = second[...]


def below_kernel(first, second, from_below, out):
    half = first.shape[1]
    out[:, :half] = first[...] + from_below[:, :half]
    out[:, half:] = second[...] + from_below[:, half:]


def last_kernel(held, from_above, out):
    x = lax.axis_index("row") // 2
    for index, t in enumerate(ORDER):
        source = pl.ds(index * 2 * TILE, 2 * TILE)
        target = pl.ds(pl.multiple_of(lax.rem(x + t, N_X) * 2 * TILE, 2 * TILE), 2 * TILE)
        out[:, target] = held[:, source] + from_above[:, source]


def swap(value):
    return lax.ppermute(value, "row", [(i, i ^ 1) for i in range(N_ROW)])


def fetch(value, t):
    pairs = []
    for x in range(N_X):
        for y in range(N_COL):
            pairs.append(((2 * x) * N_COL + (y + t) % N_COL, (2 * x) * N_COL + y))
            pairs.append(((2 * ((x + t) % N_X) + 1) * N_COL + y, (2 * x + 1) * N_COL + y))
    return lax.ppermute(value, ("row", "col"), pairs)


def pass_on(value, distance):
    pairs = []
    for z in range(N_LAYER):
        for row in range(N_ROW):
            to = (z + (distance if row % 2 == 0 else -distance)) % N_LAYER
            pairs.append((z * N_ROW + row, to * N_ROW + row))
    return lax.ppermute(value, ("layer", "row"), pairs)


def on_device(graph, pattern):
    inner = graph.shape[0]
    tiles = inner // TILE
    (masked,) = call(
        mask_kernel,
        [(inner, TILE)],
        (graph, pattern.reshape(-1)),
        [pl.BlockSpec(memory_space=pltpu.HBM)] * 2,
        scratch=[
            pltpu.VMEM((inner, TILE), F32),
            pltpu.SMEM((tiles,), jnp.int32),
            pltpu.SemaphoreType.DMA((tiles + 1,)),
            pltpu.SemaphoreType.DMA((tiles,)),
        ],
        limit=62 * 1024 * 1024,
        out_spec=pl.BlockSpec(memory_space=pltpu.HBM),
    )
    other = swap(masked)
    o1, o3 = fetch(masked, 1), fetch(masked, 3)
    s3, s1 = fetch(other, 3), fetch(other, 1)
    o2, s2 = fetch(o1, 1), fetch(s3, 3)

    def swap_two(first, second, after=None):
        return swap(call(join_kernel, [(2 * inner, TILE)], (first, second), after=after)[0])

    known, wide = 3 * TILE, 6 * TILE
    shapes = [((known, inner), BF16)] * 2 + [((inner, wide), BF16)] * 2 + [(known, wide)]
    early = call(early_product_kernel, shapes, (masked, other, o1, s1, o3, s3), nbytes=1 << 10)
    second = (o2, s2, swap_two(o2, s2, after=early[4]))
    late = call(
        first_product_kernel,
        [((known - TILE, inner), BF16)] * 2
        + [((inner, wide - 2 * TILE), BF16)] * 2
        + [(known, wide - 2 * TILE), (known - TILE, wide)],
        (swap_two(o1, s3), swap_two(o3, s1), *early[:4]),
        flops=4 * known * wide * inner,
        nbytes=8 << 20,
    )
    cut = (4 * SUB, 4 * TILE)
    total = pltpu.VMEM((4 * TILE, 4 * TILE), F32)
    mine_a, up_a, down_a, two_a, *last = call(
        second_product_kernel,
        [cut] * 4 + [((TILE, inner), BF16)] * 2,
        (*second, *early[2:], *late[2:]),
        scratch=[total],
        flops=6 * TILE * 4 * TILE * inner,
        nbytes=4 << 20,
    )
    mine_b, up_b, down_b, two_b = call(
        third_product_kernel,
        [cut] * 4,
        (*second, *last, *early, *late),
        scratch=[pltpu.VMEM((inner, 2 * TILE), BF16)] * 2 + [total],
        flops=6 * 5 * TILE * 2 * TILE * inner,
        nbytes=4 << 20,
    )
    (downs,) = call(join_kernel, [(8 * SUB, 4 * TILE)], (down_a, down_b))
    above = pass_on(downs, -1)
    (up_a,) = call(add_kernel, [cut], (up_a, pass_on(two_a, 1)))
    (up_b,) = call(add_kernel, [cut], (up_b, pass_on(two_b, 1)), after=up_a)
    piece = [(SUB, 4 * TILE)] * 4
    first = call(functools.partial(group_kernel, 0), piece, (mine_a, pass_on(up_a, 1), above))
    second = call(functools.partial(group_kernel, 1), piece, (mine_b, pass_on(up_b, 1), above), after=first[0])
    chunk = [(SUB, 8 * TILE)]
    (down,) = call(beside_kernel, chunk, (first[3], second[3]))
    (held,) = call(below_kernel, chunk, (first[0], second[0], pass_on(down, -4)))
    (up,) = call(up_kernel, chunk, (first[1], pass_on(first[2], 4), second[1], pass_on(second[2], 4)))
    return call(last_kernel, chunk, (held, pass_on(up, 4)))[0]


def solution(mesh):
    placed = (P("layer", ("row", "col")), P("layer", ("row", "col")))
    return jax.shard_map(
        on_device, mesh=mesh, in_specs=placed, out_specs=P(("row", "layer"), "col"), check_vma=False
    )
```

```python
import functools

import jax
import jax.numpy as jnp
from jax import lax
from jax.experimental import pallas as pl
from jax.experimental.pallas import tpu as pltpu
from jax.sharding import PartitionSpec as P

TILE = 128
N_LAYER = 16
N_X = 4
N_ROW = 8
N_COL = 4
SUB = 32
ORDER = (0, 1, 3, 2)
VMEM = pl.BlockSpec(memory_space=pltpu.VMEM)
SMEM = pl.BlockSpec(memory_space=pltpu.SMEM)
LIMIT = 40 * 1024 * 1024
F32, BF16 = jnp.float32, jnp.bfloat16


def call(kernel, outs, operands, specs=None, scratch=(), flops=0, nbytes=1 << 20, after=None, limit=LIMIT, out_spec=VMEM):
    if after is not None:
        inner_kernel, count = kernel, len(operands)
        kernel = lambda *refs: inner_kernel(*refs[:count], *refs[count + 1 :])
        specs = [VMEM] * count + [pl.BlockSpec(memory_space=pl.ANY)]
        operands = (*operands, after)
    outs = [o if isinstance(o[0], tuple) else (o, F32) for o in outs]
    return pl.pallas_call(
        kernel,
        out_shape=tuple(jax.ShapeDtypeStruct(s, d) for s, d in outs),
        in_specs=specs or [VMEM] * len(operands),
        out_specs=tuple(out_spec for _ in outs),
        scratch_shapes=list(scratch),
        compiler_params=pltpu.CompilerParams(vmem_limit_bytes=limit),
        cost_estimate=pl.CostEstimate(flops=flops, bytes_accessed=nbytes, transcendentals=0),
    )(*operands)


def mask_kernel(graph, pattern, masked, raw, flags, sems, out_sems):
    tiles = graph.shape[0] // TILE
    flag_copy = pltpu.make_async_copy(pattern, flags, sems.at[tiles])
    flag_copy.start()
    copies, outs = [], []
    for k in range(tiles):
        rows = pl.ds(k * TILE, TILE)
        copies.append(pltpu.make_async_copy(graph.at[rows, :], raw.at[rows, :], sems.at[k]))
        outs.append(pltpu.make_async_copy(raw.at[rows, :], masked.at[rows, :], out_sems.at[k]))
        copies[k].start()
    flag_copy.wait()
    for k in range(tiles):
        rows = pl.ds(k * TILE, TILE)
        copies[k].wait()
        raw[rows, :] = raw[rows, :] * flags[k].astype(F32)
        outs[k].start()
    for out in outs:
        out.wait()


def core():
    return lax.rem(lax.axis_index("row"), 2)


def join_kernel(first, second, pair):
    rows = first.shape[0]
    pair[:rows, :] = first[...]
    pair[rows:, :] = second[...]


def split(value):
    high = value.astype(BF16)
    low = (value - high.astype(F32)).astype(BF16)
    return high, low


dot = functools.partial(jnp.dot, preferred_element_type=F32)


def product(left_high, left_low, right_high, right_low):
    return dot(left_high, right_high) + (dot(left_high, right_low) + dot(left_low, right_high))


def take_left(index, block, left_high, left_low):
    rows = pl.ds(index * TILE, TILE)
    high, low = split(block[...].T)
    left_high[rows, :] = high
    left_low[rows, :] = low


def take_right(index, parity, block, right_high, right_low):
    start = 2 * index * TILE + parity * TILE
    columns = pl.ds(start if isinstance(start, int) else pl.multiple_of(start, TILE), TILE)
    high, low = split(block[...])
    right_high[:, columns] = high
    right_low[:, columns] = low


def halves(pair):
    inner = pair.shape[0] // 2
    return pair.at[pl.ds(0, inner), :], pair.at[pl.ds(inner, inner), :]


def early_product_kernel(own, other, o1, s1, o3, s3, left_high, left_low, right_high, right_low, total):
    left, right = (left_high, left_low), (right_high, right_low)
    take_left(0, own, *left)
    take_right(0, core(), own, *right)
    take_right(0, 1 - core(), other, *right)

    @pl.when(core() == 0)
    def _():
        take_left(1, o1, *left)
        take_left(2, o3, *left)
        columns = pl.ds(0, 2 * TILE)
        total[:, columns] = product(left_high[...], left_low[...], right_high[:, columns], right_low[:, columns])

    @pl.when(core() == 1)
    def _():
        for index, o, s in ((1, o1, s1), (2, o3, s3)):
            take_right(index, 0, s, *right)
            take_right(index, 1, o, *right)
        rows = pl.ds(0, TILE)
        total[rows, :] = product(left_high[rows, :], left_low[rows, :], right_high[...], right_low[...])


def first_product_kernel(o1_s3, o3_s1, early_left, early_left_low, early_right, early_right_low, *refs):
    left_high, left_low, right_high, right_low, beside, below = refs
    (o1, s3), (o3, s1) = halves(o1_s3), halves(o3_s1)

    @pl.when(core() == 0)
    def _():
        for index, o, s in ((0, o1, s1), (1, o3, s3)):
            take_right(index, 0, s, right_high, right_low)
            take_right(index, 1, o, right_high, right_low)
        beside[...] = product(early_left[...], early_left_low[...], right_high[...], right_low[...])

    @pl.when(core() == 1)
    def _():
        take_left(0, s1, left_high, left_low)
        take_left(1, s3, left_high, left_low)
        below[...] = product(left_high[...], left_low[...], early_right[...], early_right_low[...])


def turn():
    return 1 - 2 * core()


def strip(index):
    return pl.ds(pl.multiple_of(index * SUB, SUB), SUB)


def scatter(total, outs):
    z = lax.axis_index("layer")
    for shift, out in zip((0, 1, -1, 2), outs):
        s = lax.rem(z + turn() * shift + 4, 4)
        for index in range(4):
            out[pl.ds(index * SUB, SUB), :] = total[strip(index * 4 + s), :]


def second_product_kernel(o2, s2, both, early_right, early_right_low, early, right_high, right_low, beside, below, *refs):
    outs, (last_high, last_low, total) = refs[:4], refs[4:]
    known, wide = early.shape[0], 2 * TILE
    first, next_ = pl.ds(0, wide), pl.ds(wide, wide)

    def last_rows(columns, high, low):
        total[known:, columns] = product(last_high[...], last_low[...], high, low)

    @pl.when(core() == 0)
    def _():
        take_left(0, o2, last_high, last_low)
        total[:known, first] = early[:, first]
        total[:known, next_] = beside[:, first]
        last_rows(first, early_right[:, first], early_right_low[:, first])
        last_rows(next_, right_high[:, first], right_low[:, first])

    @pl.when(core() == 1)
    def _():
        columns = pl.ds(0, 2 * wide)
        take_left(0, both.at[pl.ds(s2.shape[0], s2.shape[0]), :], last_high, last_low)
        total[:TILE, :] = early[:TILE, columns]
        total[TILE:known, :] = below[:, columns]
        last_rows(columns, early_right[:, columns], early_right_low[:, columns])

    scatter(total, outs)


def third_product_kernel(o2, s2, both, last_high, last_low, *refs):
    early_left, early_left_low, early_right, early_right_low, early = refs[:5]
    left_high, left_low, right_high, right_low, beside, below = refs[5:11]
    outs, (far_high, far_low, total) = refs[11:15], refs[15:]
    o2_swapped, s2_swapped = halves(both)
    known, wide = early.shape[0], 2 * TILE
    first, next_, third = (pl.ds(i * wide, wide) for i in range(3))

    def far(rows, high, low):
        total[rows, next_] = product(high, low, far_high[...], far_low[...])

    @pl.when(core() == 0)
    def _():
        take_right(0, 0, s2_swapped, far_high, far_low)
        take_right(0, 1, o2_swapped, far_high, far_low)
        total[:known, first] = beside[:, next_]
        total[known:, first] = product(last_high[...], last_low[...], right_high[:, next_], right_low[:, next_])
        far(pl.ds(0, known), early_left[...], early_left_low[...])
        far(pl.ds(known, TILE), last_high[...], last_low[...])

    @pl.when(core() == 1)
    def _():
        take_right(0, 0, s2, far_high, far_low)
        take_right(0, 1, o2, far_high, far_low)
        total[:TILE, first] = early[:TILE, third]
        total[TILE:known, first] = below[:, third]
        total[known:, first] = product(last_high[...], last_low[...], early_right[:, third], early_right_low[:, third])
        far(pl.ds(0, TILE), early_left[:TILE, :], early_left_low[:TILE, :])
        far(pl.ds(TILE, known - TILE), left_high[...], left_low[...])
        far(pl.ds(known, TILE), last_high[...], last_low[...])

    scatter(total, outs)


def add_kernel(held, came, out):
    out[...] = held[...] + came[...]


def group_kernel(mine, below, above, own, up, far, down):
    group, y = lax.axis_index("layer") // 4, lax.axis_index("col")
    for i, out in enumerate((own, up, far, down)):
        t = lax.rem(group + turn() * i - y + 8, 4)
        rows = strip(jnp.where(t < 2, t, 5 - t))
        out[...] = mine[rows, :] + (below[rows, :] + above[rows, :])


def up_kernel(first, first_came, second, second_came, out):
    half = first.shape[1]
    out[:, :half] = first[...] + first_came[...]
    out[:, half:] = second[...] + second_came[...]


def beside_kernel(first, second, out):
    half = first.shape[1]
    out[:, :half] = first[...]
    out[:, half:] = second[...]


def below_kernel(first, second, from_below, out):
    half = first.shape[1]
    out[:, :half] = first[...] + from_below[:, :half]
    out[:, half:] = second[...] + from_below[:, half:]


def last_kernel(held, from_above, out):
    x = lax.axis_index("row") // 2
    for index, t in enumerate(ORDER):
        source = pl.ds(index * 2 * TILE, 2 * TILE)
        target = pl.ds(pl.multiple_of(lax.rem(x + t, N_X) * 2 * TILE, 2 * TILE), 2 * TILE)
        out[:, target] = held[:, source] + from_above[:, source]


def swap(value):
    return lax.ppermute(value, "row", [(i, i ^ 1) for i in range(N_ROW)])


def fetch(value, t):
    pairs = []
    for x in range(N_X):
        for y in range(N_COL):
            pairs.append(((2 * x) * N_COL + (y + t) % N_COL, (2 * x) * N_COL + y))
            pairs.append(((2 * ((x + t) % N_X) + 1) * N_COL + y, (2 * x + 1) * N_COL + y))
    return lax.ppermute(value, ("row", "col"), pairs)


def pass_on(value, distance):
    pairs = []
    for z in range(N_LAYER):
        for row in range(N_ROW):
            to = (z + (distance if row % 2 == 0 else -distance)) % N_LAYER
            pairs.append((z * N_ROW + row, to * N_ROW + row))
    return lax.ppermute(value, ("layer", "row"), pairs)


def on_device(graph, pattern):
    inner = graph.shape[0]
    tiles = inner // TILE
    (masked,) = call(
        mask_kernel,
        [(inner, TILE)],
        (graph, pattern.reshape(-1)),
        [pl.BlockSpec(memory_space=pltpu.HBM)] * 2,
        scratch=[
            pltpu.VMEM((inner, TILE), F32),
            pltpu.SMEM((tiles,), jnp.int32),
            pltpu.SemaphoreType.DMA((tiles + 1,)),
            pltpu.SemaphoreType.DMA((tiles,)),
        ],
        limit=62 * 1024 * 1024,
        out_spec=pl.BlockSpec(memory_space=pltpu.HBM),
    )
    other = swap(masked)
    o1, o3 = fetch(masked, 1), fetch(masked, 3)
    s3, s1 = fetch(other, 3), fetch(other, 1)
    o2, s2 = fetch(o1, 1), fetch(s3, 3)

    def swap_two(first, second, after=None):
        return swap(call(join_kernel, [(2 * inner, TILE)], (first, second), after=after)[0])

    known, wide = 3 * TILE, 6 * TILE
    shapes = [((known, inner), BF16)] * 2 + [((inner, wide), BF16)] * 2 + [(known, wide)]
    early = call(early_product_kernel, shapes, (masked, other, o1, s1, o3, s3), nbytes=1 << 10)
    second = (o2, s2, swap_two(o2, s2, after=early[4]))
    late = call(
        first_product_kernel,
        [((known - TILE, inner), BF16)] * 2
        + [((inner, wide - 2 * TILE), BF16)] * 2
        + [(known, wide - 2 * TILE), (known - TILE, wide)],
        (swap_two(o1, s3), swap_two(o3, s1), *early[:4]),
        flops=4 * known * wide * inner,
        nbytes=8 << 20,
    )
    cut = (4 * SUB, 4 * TILE)
    total = pltpu.VMEM((4 * TILE, 4 * TILE), F32)
    mine_a, up_a, down_a, two_a, *last = call(
        second_product_kernel,
        [cut] * 4 + [((TILE, inner), BF16)] * 2,
        (*second, *early[2:], *late[2:]),
        scratch=[total],
        flops=6 * TILE * 4 * TILE * inner,
        nbytes=4 << 20,
    )
    mine_b, up_b, down_b, two_b = call(
        third_product_kernel,
        [cut] * 4,
        (*second, *last, *early, *late),
        scratch=[pltpu.VMEM((inner, 2 * TILE), BF16)] * 2 + [total],
        flops=6 * 5 * TILE * 2 * TILE * inner,
        nbytes=4 << 20,
    )
    (up_a,) = call(add_kernel, [cut], (up_a, pass_on(two_a, 1)))
    (up_b,) = call(add_kernel, [cut], (up_b, pass_on(two_b, 1)), after=up_a)
    piece = [(SUB, 4 * TILE)] * 4
    first = call(group_kernel, piece, (mine_a, pass_on(up_a, 1), pass_on(down_a, -1)))
    second = call(group_kernel, piece, (mine_b, pass_on(up_b, 1), pass_on(down_b, -1)), after=first[0])
    chunk = [(SUB, 8 * TILE)]
    (down,) = call(beside_kernel, chunk, (first[3], second[3]))
    (held,) = call(below_kernel, chunk, (first[0], second[0], pass_on(down, -4)))
    (up,) = call(up_kernel, chunk, (first[1], pass_on(first[2], 4), second[1], pass_on(second[2], 4)))
    return call(last_kernel, chunk, (held, pass_on(up, 4)))[0]


def solution(mesh):
    placed = (P("layer", ("row", "col")), P("layer", ("row", "col")))
    return jax.shard_map(
        on_device, mesh=mesh, in_specs=placed, out_specs=P(("row", "layer"), "col"), check_vma=False
    )
```
